32 devices in a mesh: ctx: 8 (over y, x, core), ch: 4 (over z).
Axes of the slice: x: 2, y: 2, z: 4, core: 2. Of those that a mesh axis runs over, the one named last changes fastest.
Arguments:
- q_vals: bfloat16 [8192, 2048], P('ch', 'ctx'), may hold values from -6 to 6
- k_vals: bfloat16 [8192, 2048], P('ch', 'ctx'), may hold values from -6 to 6
- v_vals: bfloat16 [8192, 2048], P('ch', 'ctx'), may hold values from -6 to 6
- grad_out: bfloat16 [8192, 2048], P('ch', 'ctx'), may hold values from -6 to 6
- exponents: int32 [3, 64, 16], P(None, 'ch', 'ctx'), may hold values from -2 to 1
- filter_taps: float32 [512, 1024], P('ch'), may hold values from -1 to 1
Outputs:
- grad_q: bfloat16 [8192, 2048], P('ch', 'ctx')
- grad_k: bfloat16 [8192, 2048], P('ch', 'ctx')
- grad_v: bfloat16 [8192, 2048], P('ch', 'ctx')
- grad_filter: float32 [512, 1024], P('ch', 'ctx')
- grad_amax: float32 [3, 16], P(None, 'ctx')
The draws below stay inside these ranges and needn't reach their ends.
All inputs are finite; a program needn't handle non-finite values.
Results may differ from the reference program's by a relative error of at most 0.0061.
Values may be sent and summed in bfloat16 or wider, within the bound.
A program may use at most 128 MiB of HBM per device.

```python
import math
import jax
import jax.numpy as jnp
from jax import lax

D = 8192
FILTER_GROUPS = 512
QB = 128
SEQ = 2048
FILTER_TAP_COUNT = 1024


def draw_filter_taps(key, part):
    random_key_list = jax.random.split(jax.random.fold_in(key, 7), 7)
    slow_share = 0.5
    magnitude = jax.random.uniform(random_key_list[5], (FILTER_GROUPS, FILTER_TAP_COUNT), jnp.float32, 0.5, 1.5)
    slow = jax.random.bernoulli(random_key_list[0], slow_share, (FILTER_GROUPS, 1))
    fast_len = jax.random.uniform(random_key_list[1], (FILTER_GROUPS, 1), jnp.float32, 30.0, 50.0)
    slow_len = jnp.exp(jax.random.uniform(random_key_list[2], (FILTER_GROUPS, 1), jnp.float32, math.log(FILTER_TAP_COUNT * 1.0), math.log(FILTER_TAP_COUNT * 4.0)))
    length = jnp.where(slow, slow_len, fast_len)
    lag_location = jnp.arange(FILTER_TAP_COUNT, dtype=jnp.float32)[None, :]
    decay_profile = jnp.exp(-lag_location / length)
    spike_location = jax.random.randint(random_key_list[3], (FILTER_GROUPS, 2), 0, FILTER_TAP_COUNT).astype(jnp.float32)
    spike_retained = jax.random.uniform(random_key_list[4], (FILTER_GROUPS, 2), jnp.float32, 0.55, 0.8)
    for selected_variant in range(2):
        decay_profile = decay_profile * jnp.where(lag_location >= spike_location[:, selected_variant:selected_variant + 1], spike_retained[:, selected_variant:selected_variant + 1], 1.0)
    signs = jnp.where(jax.random.bernoulli(random_key_list[6], 0.5, (FILTER_GROUPS, FILTER_TAP_COUNT)), 1.0, -1.0)
    amplitude = jnp.sqrt(2.0 / length)
    return (amplitude * decay_profile * magnitude * signs).astype(jnp.float32)


def with_ends(entries, key, least, high):
    longest = entries.shape.index(max(entries.shape))
    spots = []
    for shift in (0, 1):
        where = [jax.random.randint(jax.random.fold_in(key, axis), (), 0, length) for axis, length in enumerate(entries.shape)]
        where[longest] = (where[longest] + shift) % entries.shape[longest]
        spots.append(tuple(where))
    return entries.at[spots[0]].set(least).at[spots[1]].set(high)


def level_of(stream_key, dims, cuts, smallest, top_value):
    gain = 1.0
    for dim, parts in cuts:
        steps = jax.random.uniform(jax.random.fold_in(jax.random.fold_in(stream_key, 6), dim), (parts,), jnp.float32, smallest / len(cuts), top_value / len(cuts))
        gain = gain * jnp.repeat(jnp.exp(steps), dims[dim] // parts).reshape((-1,) + (1,) * (len(dims) - 1 - dim))
    return gain


def gaussian(key, shape, width, reach, cuts=(), kind=jnp.bfloat16):
    loudness = level_of(key, shape, cuts, -0.22, 0.18) if cuts else 1.0
    values = jax.random.normal(key, shape, jnp.float32) * width * loudness
    return jnp.minimum(jnp.maximum(values, -reach), reach).astype(kind)


def setup_inputs(seed: int = 0) -> dict:
    key_of = jax.random.split(jax.random.key(seed), 7)
    q_vals = gaussian(key_of[0], (D, SEQ), 1.0, 6.0, ((0, 4), (1, 8)))
    k_vals = gaussian(key_of[1], (D, SEQ), 1.0, 6.0, ((0, 4), (1, 8)))
    v_vals = gaussian(key_of[2], (D, SEQ), 1.0, 6.0, ((0, 4), (1, 8)))
    grad_out = gaussian(key_of[3], (D, SEQ), 1.0, 6.0, ((0, 4), (1, 8)))
    exponents = with_ends(jax.random.randint(key_of[4], (3, D // QB, SEQ // QB), -2, 2), jax.random.fold_in(key_of[4], 1), -2, 1).astype(jnp.int32)
    filter_taps = draw_filter_taps(jax.random.fold_in(key_of[6], 71), 0)
    return dict(q_vals=q_vals, k_vals=k_vals, v_vals=v_vals, grad_out=grad_out, exponents=exponents, filter_taps=filter_taps)


EPS = 1e-6


def reference(q_vals, k_vals, v_vals, grad_out, exponents, filter_taps):
    group_width = D // FILTER_GROUPS
    slab_width = D // 16
    slab_groups = FILTER_GROUPS // 16
    scales = jnp.exp2(exponents.astype(jnp.float32))
    scales = scales.reshape(3, 16, slab_width // QB, SEQ // QB).transpose(1, 0, 2, 3)
    taps = lax.optimization_barrier(filter_taps.astype(jnp.bfloat16)).astype(jnp.float32)
    padded = jnp.pad(taps, ((0, 0), (0, SEQ - FILTER_TAP_COUNT))).reshape(16, slab_groups, SEQ)

    def expand(scale):
        return jnp.repeat(jnp.repeat(scale, QB, axis=0), QB, axis=1)

    def one_slab(pieces):
        q_part, k_part, v_part, g_part, scale_part, tap_part = pieces
        q_real = q_part.astype(jnp.float32) * expand(scale_part[0])
        k_real = k_part.astype(jnp.float32) * expand(scale_part[1])
        v_real = v_part.astype(jnp.float32) * expand(scale_part[2])
        gated = lax.optimization_barrier((k_real * v_real).astype(jnp.bfloat16)).astype(jnp.float32)
        grad_mix = lax.optimization_barrier((q_real * g_part.astype(jnp.float32)).astype(jnp.bfloat16)).astype(jnp.float32)
        per_channel = jnp.repeat(tap_part, group_width, axis=0)
        z_freq = jnp.fft.rfft(gated, axis=1)
        h_freq = jnp.fft.rfft(per_channel, axis=1)
        g_freq = jnp.fft.rfft(grad_mix, axis=1)
        conv_out = jnp.fft.irfft(z_freq * h_freq, n=SEQ, axis=1)
        grad_z = jnp.fft.irfft(g_freq * jnp.conj(h_freq), n=SEQ, axis=1)
        correl = jnp.fft.irfft(g_freq * jnp.conj(z_freq), n=SEQ, axis=1)
        grad_taps = correl.reshape(slab_groups, group_width, SEQ).sum(axis=1)[:, :FILTER_TAP_COUNT]
        grad_gate = g_part.astype(jnp.float32) * conv_out
        return grad_gate, grad_z * v_real, grad_z * k_real, grad_taps

    grad_gate, grad_key, grad_value, grad_taps = lax.map(
        one_slab,
        (q_vals.reshape(16, slab_width, SEQ), k_vals.reshape(16, slab_width, SEQ),
         v_vals.reshape(16, slab_width, SEQ), grad_out.reshape(16, slab_width, SEQ),
         scales, padded))
    grad_gate = grad_gate.reshape(D, SEQ)
    grad_key = grad_key.reshape(D, SEQ)
    grad_value = grad_value.reshape(D, SEQ)
    grad_filter = grad_taps.reshape(FILTER_GROUPS, FILTER_TAP_COUNT)

    def block_max(values):
        return jnp.max(jnp.abs(values).reshape(D, SEQ // QB, QB), axis=(0, 2))

    grad_amax = jnp.stack([block_max(grad_gate), block_max(grad_key), block_max(grad_value)])

    def scaled(values, peak):
        return (values / (jnp.repeat(peak, QB) + EPS)[None, :]).astype(jnp.bfloat16)

    return (scaled(grad_gate, grad_amax[0]), scaled(grad_key, grad_amax[1]),
            scaled(grad_value, grad_amax[2]), grad_filter, grad_amax)
```

```python
import functools

import jax
import jax.numpy as jnp
from jax import lax
from jax.experimental import pallas as pl
from jax.experimental.pallas import tpu as pltpu
from jax.sharding import PartitionSpec as P

EPS = 1e-06
MESH = pl.DeviceIdType.MESH
CHUNKS = 4
HALF = 128


def exchange_kernel(
    n, m, group_width, scale_rows, blocks,
    q_ref, k_ref, v_ref, g_ref, sc_ref, taps_ref,
    conv_out, filt_out, peak_out,
    zs, zf, ws, wr, tt, gfs, gfr, peak, pks,
    in_send, in_recv, back_send, back_recv, out_sem, gf_send, gf_recv, pk_send, pk_recv,
):
    me = lax.axis_index("ctx")
    row_me = lax.axis_index("ch")
    channels, rows = q_ref.shape
    own = channels // n
    chunk = own // CHUNKS
    own_groups = own // group_width
    chunk_groups = own_groups // CHUNKS
    scale_blocks = channels // scale_rows
    filter_len = taps_ref.shape[1]
    lead = filter_len // rows
    cols = filter_len // n
    width = filter_len + HALF
    f32 = jnp.float32

    barrier = pltpu.get_barrier_semaphore()

    def greet_ctx(i, c):
        pl.semaphore_signal(
            barrier, inc=1, device_id={"ctx": lax.rem(me + i, n)}, device_id_type=MESH
        )
        return c

    def greet_ch(i, c):
        pl.semaphore_signal(
            barrier, inc=1, device_id={"ch": lax.rem(row_me + i, m)}, device_id_type=MESH
        )
        return c

    lax.fori_loop(1, n, greet_ctx, 0)
    lax.fori_loop(1, m, greet_ch, 0)

    def at_rows(owner, j):
        return pl.ds(pl.multiple_of(owner * own + j * chunk, 16), chunk)

    def scale_of(which, owner, j):
        return sc_ref[which * scale_blocks + (owner * own + j * chunk) // scale_rows]

    def real(ref, which, owner, j):
        return ref[at_rows(owner, j), :].astype(f32) * scale_of(which, owner, j)

    def mixed(owner, j):
        z = (real(k_ref, 1, owner, j) * real(v_ref, 2, owner, j)).astype(jnp.bfloat16)
        gw = (real(q_ref, 0, owner, j) * g_ref[at_rows(owner, j), :].astype(f32)).astype(jnp.bfloat16)
        return z, gw

    def in_copy(j, dst, src):
        return pltpu.make_async_remote_copy(
            src_ref=zs.at[:, at_rows(dst, j), :],
            dst_ref=zf.at[src, :, pl.ds(pl.multiple_of(j * chunk, 16), chunk), :],
            send_sem=in_send.at[j, dst],
            recv_sem=in_recv.at[j, src],
            device_id={"ctx": dst},
            device_id_type=MESH,
        )

    def back_copy(j, dst, src):
        return pltpu.make_async_remote_copy(
            src_ref=ws.at[dst, :, pl.ds(pl.multiple_of(j * chunk, 16), chunk), :],
            dst_ref=wr.at[:, at_rows(src, j), :],
            send_sem=back_send.at[j, dst],
            recv_sem=back_recv.at[j, src],
            device_id={"ctx": dst},
            device_id_type=MESH,
        )

    def gf_copy(dst, src):
        return pltpu.make_async_remote_copy(
            src_ref=gfs.at[dst],
            dst_ref=gfr.at[src],
            send_sem=gf_send.at[dst],
            recv_sem=gf_recv.at[src],
            device_id={"ctx": dst},
            device_id_type=MESH,
        )

    def pk_copy(dst, src):
        return pltpu.make_async_remote_copy(
            src_ref=pks.at[row_me],
            dst_ref=pks.at[src],
            send_sem=pk_send.at[dst],
            recv_sem=pk_recv.at[src],
            device_id={"ch": dst},
            device_id_type=MESH,
        )

    def out_copy(j, owner):
        return pltpu.make_async_copy(
            wr.at[:, at_rows(owner, j), :], conv_out.at[:, at_rows(owner, j), :], out_sem.at[j, owner]
        )

    pl.semaphore_wait(barrier, n - 1 + m - 1)

    def send_chunk(j, c):
        def one(i, c):
            dst = lax.rem(me + i, n)
            z, gw = mixed(dst, j)
            zs[0, at_rows(dst, j), :] = z
            zs[1, at_rows(dst, j), :] = gw
            in_copy(j, dst, me).start()
            return c

        lax.fori_loop(1, n, one, 0)
        z, gw = mixed(me, j)
        here = pl.ds(pl.multiple_of(j * chunk, 16), chunk)
        zf[me, 0, here, :] = z
        zf[me, 1, here, :] = gw
        return c

    lax.fori_loop(0, CHUNKS, send_chunk, 0)

    peak[...] = jnp.zeros_like(peak)
    flip = (
        lax.broadcasted_iota(jnp.int32, (HALF, HALF), 0)
        + lax.broadcasted_iota(jnp.int32, (HALF, HALF), 1)
        == HALF - 1
    ).astype(f32).astype(jnp.bfloat16)
    zero = jnp.zeros((HALF, HALF), jnp.bfloat16)

    def turned(x, by):
        by = (by * group_width) % x.shape[0]
        return x if by == 0 else jnp.concatenate([x[-by:], x[:-by]], axis=0)

    def one_group(gi, c):
        at = pl.ds(pl.multiple_of(gi * group_width, 16), group_width)
        z = zf[:, 0, at, :].reshape(n * group_width, rows)
        gw = zf[:, 1, at, :].reshape(n * group_width, rows)
        taps = taps_ref[pl.ds(me * own_groups + gi, 1), :].astype(jnp.bfloat16).astype(f32)
        line = jnp.concatenate([taps, jnp.zeros((1, HALF), f32)], axis=1)
        band = pltpu.roll(
            jnp.broadcast_to(line, (HALF, width)), 0, 1, stride=1, stride_axis=0
        ).astype(jnp.bfloat16)

        def tile(i):
            if i < 0 or i * HALF >= width:
                return zero
            return band[:, i * HALF : (i + 1) * HALF]

        per = rows // HALF
        for o in range(lead + 1):
            for a in range(per):
                for b in range(per):
                    tt[o * rows + a * HALF : o * rows + (a + 1) * HALF, b * HALF : (b + 1) * HALF] = tile(
                        o * per + b - a
                    )
        zwin = jnp.concatenate([turned(z, o) for o in range(lead + 1)], axis=1)
        w = jnp.dot(zwin, tt[...], preferred_element_type=f32)
        gparts = [turned(gw, -o) for o in range(lead + 1)]
        gz = jnp.zeros((n * group_width, rows), f32)
        for o in range(lead + 1):
            gz = gz + lax.dot_general(
                gparts[o], tt[o * rows : (o + 1) * rows, :], (((1,), (1,)), ((), ())),
                preferred_element_type=f32,
            )
        ws[:, 0, at, :] = w.astype(jnp.bfloat16).reshape(n, group_width, rows)
        ws[:, 1, at, :] = gz.astype(jnp.bfloat16).reshape(n, group_width, rows)

        gwin = jnp.concatenate(gparts, axis=1)
        zcat = jnp.concatenate([z[:, a * HALF : (a + 1) * HALF] for a in range(per)], axis=0)
        gcat = jnp.concatenate([gwin[:, a * HALF : a * HALF + width] for a in range(per)], axis=0)
        zrev = lax.dot_general(
            flip, zcat, (((1,), (1,)), ((), ())), preferred_element_type=f32
        ).astype(jnp.bfloat16)
        cross = jnp.dot(zrev, gcat, preferred_element_type=f32)
        skewed = pltpu.roll(cross, width - (HALF - 1), 1, stride=1, stride_axis=0)
        lags = jnp.sum(skewed, axis=0, keepdims=True)
        for d in range(n):
            gfs[d, pl.ds(gi, 1), :] = lags[:, d * cols : (d + 1) * cols]
        return c

    def note_peak(j, owner):
        conv = wr[0, at_rows(owner, j), :].astype(f32)
        gz = wr[1, at_rows(owner, j), :].astype(f32)
        gq = g_ref[at_rows(owner, j), :].astype(f32) * conv
        gk = gz * real(v_ref, 2, owner, j)
        gv = gz * real(k_ref, 1, owner, j)
        for i, x in enumerate((gq, gk, gv)):
            peak[i] = jnp.maximum(peak[i], jnp.max(jnp.abs(x).reshape(chunk // 8, 8, rows), axis=0))

    def take_back(j):
        def one(i, c):
            src = lax.rem(me + n - i, n)
            back_copy(j, me, src).wait_recv()
            out_copy(j, src).start()
            note_peak(j, src)
            return c

        lax.fori_loop(1, n, one, 0)
        out_copy(j, me).start()
        note_peak(j, me)

    def work_chunk(j, c):
        def arrive(i, c):
            src = lax.rem(me + n - i, n)
            in_copy(j, me, src).wait_recv()
            return c

        lax.fori_loop(1, n, arrive, 0)
        lax.fori_loop(j * chunk_groups, (j + 1) * chunk_groups, one_group, 0)

        def reply(i, c):
            back_copy(j, lax.rem(me + i, n), me).start()
            return c

        lax.fori_loop(1, n, reply, 0)
        here = pl.ds(pl.multiple_of(j * chunk, 16), chunk)
        for i in range(2):
            wr[i, at_rows(me, j), :] = ws[me, i, here, :]
        return c

    lax.fori_loop(0, CHUNKS, work_chunk, 0)

    def send_gf(i, c):
        gf_copy(lax.rem(me + i, n), me).start()
        return c

    lax.fori_loop(1, n, send_gf, 0)

    def take_chunk(j, c):
        take_back(j)
        return c

    lax.fori_loop(0, CHUNKS, take_chunk, 0)

    for i in range(3):
        lanes = jnp.max(peak[i], axis=0, keepdims=True)
        per = rows // blocks
        pks[row_me, i : i + 1, :] = jnp.concatenate(
            [
                jnp.broadcast_to(jnp.max(lanes[:, b * per : (b + 1) * per], axis=1, keepdims=True), (1, per))
                for b in range(blocks)
            ],
            axis=1,
        )
    pks[row_me, 3:8, :] = jnp.zeros((5, rows), f32)

    def send_pk(i, c):
        pk_copy(lax.rem(row_me + i, m), row_me).start()
        return c

    lax.fori_loop(1, m, send_pk, 0)

    gfr[me] = gfs[me]

    def settle_ctx(i, c):
        dst = lax.rem(me + i, n)
        src = lax.rem(me + n - i, n)
        gf_copy(me, src).wait_recv()
        gf_copy(dst, me).wait_send()

        def both(j, c):
            in_copy(j, dst, me).wait_send()
            back_copy(j, dst, me).wait_send()
            return c

        lax.fori_loop(0, CHUNKS, both, 0)
        return c

    lax.fori_loop(1, n, settle_ctx, 0)
    filt_out[...] = gfr[...]

    def settle_ch(i, c):
        pk_copy(row_me, lax.rem(row_me + m - i, m)).wait_recv()
        pk_copy(lax.rem(row_me + i, m), row_me).wait_send()
        return c

    lax.fori_loop(1, m, settle_ch, 0)
    peak_out[...] = jnp.max(pks[...], axis=0)

    def settle_out(j, c):
        def one(i, c):
            out_copy(j, i).wait()
            return c

        lax.fori_loop(0, n, one, 0)
        return c

    lax.fori_loop(0, CHUNKS, settle_out, 0)


def scale_kernel(scale_rows, conv_ref, g_ref, k_ref, v_ref, sc_ref, peak_ref, oq, ok, ov):
    f32 = jnp.float32
    inv = 1.0 / (peak_ref[0:3, :] + EPS)
    conv = conv_ref[0].astype(f32)
    gz = conv_ref[1].astype(f32)
    oq[...] = (g_ref[...].astype(f32) * conv * inv[0:1]).astype(jnp.bfloat16)
    for b in range(g_ref.shape[0] // scale_rows):
        at = slice(b * scale_rows, (b + 1) * scale_rows)
        part = gz[at]
        ok[at, :] = (part * (v_ref[at, :].astype(f32) * sc_ref[1, b]) * inv[1:2]).astype(jnp.bfloat16)
        ov[at, :] = (part * (k_ref[at, :].astype(f32) * sc_ref[0, b]) * inv[2:3]).astype(jnp.bfloat16)


def shards(n, m, q_vals, k_vals, v_vals, grad_out, exponents, filter_taps):
    channels, rows = q_vals.shape
    groups, filter_len = filter_taps.shape
    _, scale_blocks, blocks = exponents.shape
    scale_rows = channels // scale_blocks
    group_width = channels // groups
    own = channels // n
    own_groups = groups // n
    cols = filter_len // n
    lead = filter_len // rows
    bf16, f32 = jnp.bfloat16, jnp.float32
    scales = jnp.repeat(jnp.exp2(exponents.astype(f32)), rows // blocks, axis=2)
    vmem = pl.BlockSpec(memory_space=pltpu.VMEM)
    dma = pltpu.SemaphoreType.DMA
    conv, filt, peak = pl.pallas_call(
        functools.partial(exchange_kernel, n, m, group_width, scale_rows, blocks),
        out_shape=(
            jax.ShapeDtypeStruct((2, channels, rows), bf16),
            jax.ShapeDtypeStruct((n, own_groups, cols), f32),
            jax.ShapeDtypeStruct((8, rows), f32),
        ),
        in_specs=[vmem] * 6,
        out_specs=(pl.BlockSpec(memory_space=pl.ANY), vmem, vmem),
        scratch_shapes=[
            pltpu.VMEM((2, channels, rows), bf16),
            pltpu.VMEM((n, 2, own, rows), bf16),
            pltpu.VMEM((n, 2, own, rows), bf16),
            pltpu.VMEM((2, channels, rows), bf16),
            pltpu.VMEM(((lead + 1) * rows, rows), bf16),
            pltpu.VMEM((n, own_groups, cols), f32),
            pltpu.VMEM((n, own_groups, cols), f32),
            pltpu.VMEM((3, 8, rows), f32),
            pltpu.VMEM((m, 8, rows), f32),
            dma((CHUNKS, n)),
            dma((CHUNKS, n)),
            dma((CHUNKS, n)),
            dma((CHUNKS, n)),
            dma((CHUNKS, n)),
            dma((n,)),
            dma((n,)),
            dma((m,)),
            dma((m,)),
        ],
        compiler_params=pltpu.CompilerParams(
            collective_id=0, has_side_effects=True, vmem_limit_bytes=48 * 1024 * 1024
        ),
    )(
        q_vals, k_vals, v_vals, grad_out,
        scales.reshape(3 * scale_blocks, 1, rows), filter_taps,
    )
    tile = min(256, channels)
    flat = pl.BlockSpec((tile, rows), lambda i: (i, 0))
    grads = pl.pallas_call(
        functools.partial(scale_kernel, scale_rows),
        grid=(channels // tile,),
        out_shape=tuple(jax.ShapeDtypeStruct((channels, rows), bf16) for _ in range(3)),
        in_specs=[
            pl.BlockSpec((2, tile, rows), lambda i: (0, i, 0)),
            flat, flat, flat,
            pl.BlockSpec((2, tile // scale_rows, 1, rows), lambda i: (0, i, 0, 0)),
            pl.BlockSpec((8, rows), lambda i: (0, 0)),
        ],
        out_specs=(flat, flat, flat),
    )(conv, grad_out, k_vals, v_vals, scales[1:3].reshape(2, scale_blocks, 1, rows), peak)
    return (*grads, filt.reshape(groups, cols), peak[0:3, :: rows // blocks])


def solution(mesh):
    in_specs = (
        P("ch", "ctx"),
        P("ch", "ctx"),
        P("ch", "ctx"),
        P("ch", "ctx"),
        P(None, "ch", "ctx"),
        P("ch", None),
    )
    out_specs = (P("ch", "ctx"), P("ch", "ctx"), P("ch", "ctx"), P("ch", "ctx"), P(None, "ctx"))
    body = functools.partial(shards, mesh.shape["ctx"], mesh.shape["ch"])
    return jax.shard_map(body, mesh=mesh, in_specs=in_specs, out_specs=out_specs, check_vma=False)
```

```python
import functools

import jax
import jax.numpy as jnp
from jax import lax
from jax.experimental import pallas as pl
from jax.experimental.pallas import tpu as pltpu
from jax.sharding import PartitionSpec as P

EPS = 1e-06
MESH = pl.DeviceIdType.MESH
MOST_CHUNKS = 8
HALF = 128


def exchange_kernel(
    n, m, chunks, group_width, scale_rows, scale_blocks, blocks,
    q_in, k_in, v_in, g_in, ex_in, taps_in,
    prod_out, filt_out, peak_out,
    q_ref, k_ref, v_ref, g_ref, ex_ref, taps_ref, sc_ref,
    zs, zf, ws, wr, tt0, tt1, gfs, gfr, peak, pks,
    load_sem, small_sem,
    in_send, in_recv, back_send, back_recv, gf_send, gf_recv, pk_send, pk_recv,
):
    me = lax.axis_index("ctx")
    row_me = lax.axis_index("ch")
    _, own, rows = q_ref.shape
    chunk = own // chunks
    own_groups = own // group_width
    chunk_groups = own_groups // chunks
    filter_len = taps_ref.shape[1]
    lead = filter_len // rows
    cols = filter_len // n
    width = filter_len + HALF
    f32 = jnp.float32

    loads = tuple(zip((k_in, v_in, q_in, g_in), (k_ref, v_ref, q_ref, g_ref)))

    def load_copy(i, j):
        part = pl.ds(pl.multiple_of(j * chunk, 16), chunk)
        src, dst = loads[i]
        return pltpu.make_async_copy(src.at[:, part, :], dst.at[:, part, :], load_sem.at[i, j])

    ex_copy = pltpu.make_async_copy(ex_in, ex_ref, small_sem.at[0])
    taps_copy = pltpu.make_async_copy(taps_in.at[me], taps_ref, small_sem.at[1])
    ex_copy.start()

    def load_chunk(j, c):
        for i in range(4):
            load_copy(i, j).start()
        return c

    barrier = pltpu.get_barrier_semaphore()

    def greet_ctx(i, c):
        pl.semaphore_signal(
            barrier, inc=1, device_id={"ctx": lax.rem(me + i, n)}, device_id_type=MESH
        )
        return c

    def greet_ch(i, c):
        pl.semaphore_signal(
            barrier, inc=1, device_id={"ch": lax.rem(row_me + i, m)}, device_id_type=MESH
        )
        return c

    lax.fori_loop(1, n, greet_ctx, 0)
    lax.fori_loop(1, m, greet_ch, 0)
    lax.fori_loop(0, chunks, load_chunk, 0)
    taps_copy.start()
    ex_copy.wait()
    per_scale = rows // blocks
    for a in range(3):
        scale = jnp.exp2(ex_ref[a].astype(f32))
        for i in range(scale_blocks):
            sc_ref[a * scale_blocks + i] = jnp.concatenate(
                [jnp.broadcast_to(scale[b : b + 1, i : i + 1], (1, per_scale)) for b in range(blocks)], axis=1
            )

    def at_rows(owner, j):
        return pl.ds(pl.multiple_of(owner * own + j * chunk, 16), chunk)

    def at_part(j):
        return pl.ds(pl.multiple_of(j * chunk, 16), chunk)

    def scale_of(which, owner, j):
        return sc_ref[which * scale_blocks + (owner * own + j * chunk) // scale_rows]

    def real(ref, which, owner, j):
        return ref[owner, at_part(j), :].astype(f32) * scale_of(which, owner, j)

    def mixed(owner, j):
        z = (real(k_ref, 1, owner, j) * real(v_ref, 2, owner, j)).astype(jnp.bfloat16)
        gw = (real(q_ref, 0, owner, j) * g_ref[owner, at_part(j), :].astype(f32)).astype(jnp.bfloat16)
        return z, gw

    def in_copy(j, dst, src):
        return pltpu.make_async_remote_copy(
            src_ref=zs.at[:, at_rows(dst, j), :],
            dst_ref=zf.at[src, :, pl.ds(pl.multiple_of(j * chunk, 16), chunk), :],
            send_sem=in_send.at[j, dst],
            recv_sem=in_recv.at[j, src],
            device_id={"ctx": dst},
            device_id_type=MESH,
        )

    def back_copy(j, dst, src):
        return pltpu.make_async_remote_copy(
            src_ref=ws.at[dst, :, pl.ds(pl.multiple_of(j * chunk, 16), chunk), :],
            dst_ref=wr.at[:, at_rows(src, j), :],
            send_sem=back_send.at[j, dst],
            recv_sem=back_recv.at[j, src],
            device_id={"ctx": dst},
            device_id_type=MESH,
        )

    def gf_copy(dst, src):
        return pltpu.make_async_remote_copy(
            src_ref=gfs.at[dst],
            dst_ref=gfr.at[src],
            send_sem=gf_send.at[dst],
            recv_sem=gf_recv.at[src],
            device_id={"ctx": dst},
            device_id_type=MESH,
        )

    def pk_copy(dst, src):
        return pltpu.make_async_remote_copy(
            src_ref=pks.at[row_me],
            dst_ref=pks.at[src],
            send_sem=pk_send.at[dst],
            recv_sem=pk_recv.at[src],
            device_id={"ch": dst},
            device_id_type=MESH,
        )

    pl.semaphore_wait(barrier, n - 1 + m - 1)

    def send_chunk(j, c):
        for i in range(4):
            load_copy(i, j).wait()

        def one(i, c):
            dst = lax.rem(me + i, n)
            z, gw = mixed(dst, j)
            zs[0, at_rows(dst, j), :] = z
            zs[1, at_rows(dst, j), :] = gw
            in_copy(j, dst, me).start()
            return c

        lax.fori_loop(1, n, one, 0)
        z, gw = mixed(me, j)
        here = pl.ds(pl.multiple_of(j * chunk, 16), chunk)
        zf[me, 0, here, :] = z
        zf[me, 1, here, :] = gw
        return c

    lax.fori_loop(0, chunks, send_chunk, 0)

    taps_copy.wait()
    peak[...] = jnp.zeros_like(peak)
    flip = (
        lax.broadcasted_iota(jnp.int32, (HALF, HALF), 0)
        + lax.broadcasted_iota(jnp.int32, (HALF, HALF), 1)
        == HALF - 1
    ).astype(f32).astype(jnp.bfloat16)
    zero = jnp.zeros((HALF, HALF), jnp.bfloat16)

    def turned(x, by):
        by = (by * group_width) % x.shape[0]
        return x if by == 0 else jnp.concatenate([x[-by:], x[:-by]], axis=0)

    def one_group(gi, tt):
        at = pl.ds(pl.multiple_of(gi * group_width, 16), group_width)
        z = zf[:, 0, at, :].reshape(n * group_width, rows)
        gw = zf[:, 1, at, :].reshape(n * group_width, rows)
        taps = taps_ref[pl.ds(gi, 1), :].astype(jnp.bfloat16).astype(f32)
        line = jnp.concatenate([taps, jnp.zeros((1, HALF), f32)], axis=1)
        band = pltpu.roll(
            jnp.broadcast_to(line, (HALF, width)), 0, 1, stride=1, stride_axis=0
        ).astype(jnp.bfloat16)

        def tile(i):
            if i < 0 or i * HALF >= width:
                return zero
            return band[:, i * HALF : (i + 1) * HALF]

        per = rows // HALF
        for o in range(lead + 1):
            for a in range(per):
                for b in range(per):
                    tt[o * rows + a * HALF : o * rows + (a + 1) * HALF, b * HALF : (b + 1) * HALF] = tile(
                        o * per + b - a
                    )
        zwin = jnp.concatenate([turned(z, o) for o in range(lead + 1)], axis=1)
        w = jnp.dot(zwin, tt[...], preferred_element_type=f32)
        gparts = [turned(gw, -o) for o in range(lead + 1)]
        gz = jnp.zeros((n * group_width, rows), f32)
        for o in range(lead + 1):
            gz = gz + lax.dot_general(
                gparts[o], tt[o * rows : (o + 1) * rows, :], (((1,), (1,)), ((), ())),
                preferred_element_type=f32,
            )
        ws[:, 0, at, :] = w.astype(jnp.bfloat16).reshape(n, group_width, rows)
        ws[:, 1, at, :] = gz.astype(jnp.bfloat16).reshape(n, group_width, rows)

        gwin = jnp.concatenate(gparts, axis=1)
        zcat = jnp.concatenate([z[:, a * HALF : (a + 1) * HALF] for a in range(per)], axis=0)
        gcat = jnp.concatenate([gwin[:, a * HALF : a * HALF + width] for a in range(per)], axis=0)
        zrev = lax.dot_general(
            flip, zcat, (((1,), (1,)), ((), ())), preferred_element_type=f32
        ).astype(jnp.bfloat16)
        cross = jnp.dot(zrev, gcat, preferred_element_type=f32)
        skewed = pltpu.roll(cross, width - (HALF - 1), 1, stride=1, stride_axis=0)
        lags = jnp.sum(skewed, axis=0, keepdims=True)
        for d in range(n):
            gfs[d, pl.ds(gi, 1), :] = lags[:, d * cols : (d + 1) * cols]

    def note_peak(j, owner):
        conv = wr[0, at_rows(owner, j), :].astype(f32)
        gz = wr[1, at_rows(owner, j), :].astype(f32)
        gq = g_ref[owner, at_part(j), :].astype(f32) * conv
        gk = gz * real(v_ref, 2, owner, j)
        gv = gz * real(k_ref, 1, owner, j)
        for i, x in enumerate((gq, gk, gv)):
            prod_out[i, at_rows(owner, j), :] = x
            peak[i] = jnp.maximum(peak[i], jnp.max(jnp.abs(x).reshape(chunk // 8, 8, rows), axis=0))

    def take_back(j):
        def one(i, c):
            src = lax.rem(me + n - i, n)
            back_copy(j, me, src).wait_recv()
            note_peak(j, src)
            return c

        lax.fori_loop(1, n, one, 0)
        note_peak(j, me)

    def work_chunk(j, c):
        def arrive(i, c):
            src = lax.rem(me + n - i, n)
            in_copy(j, me, src).wait_recv()
            return c

        lax.fori_loop(1, n, arrive, 0)
        for u in range(chunk_groups):
            one_group(j * chunk_groups + u, tt1 if u % 2 else tt0)

        def reply(i, c):
            back_copy(j, lax.rem(me + i, n), me).start()
            return c

        lax.fori_loop(1, n, reply, 0)
        here = pl.ds(pl.multiple_of(j * chunk, 16), chunk)
        for i in range(2):
            wr[i, at_rows(me, j), :] = ws[me, i, here, :]
        return c

    lax.fori_loop(0, chunks, work_chunk, 0)

    def send_gf(i, c):
        gf_copy(lax.rem(me + i, n), me).start()
        return c

    lax.fori_loop(1, n, send_gf, 0)

    def take_chunk(j, c):
        take_back(j)
        return c

    lax.fori_loop(0, chunks, take_chunk, 0)

    for i in range(3):
        lanes = jnp.max(peak[i], axis=0, keepdims=True)
        per = rows // blocks
        pks[row_me, i : i + 1, :] = jnp.concatenate(
            [
                jnp.broadcast_to(jnp.max(lanes[:, b * per : (b + 1) * per], axis=1, keepdims=True), (1, per))
                for b in range(blocks)
            ],
            axis=1,
        )
    pks[row_me, 3:8, :] = jnp.zeros((5, rows), f32)

    def send_pk(i, c):
        pk_copy(lax.rem(row_me + i, m), row_me).start()
        return c

    lax.fori_loop(1, m, send_pk, 0)

    gfr[me] = gfs[me]

    def settle_ctx(i, c):
        dst = lax.rem(me + i, n)
        src = lax.rem(me + n - i, n)
        gf_copy(me, src).wait_recv()
        gf_copy(dst, me).wait_send()

        def both(j, c):
            in_copy(j, dst, me).wait_send()
            back_copy(j, dst, me).wait_send()
            return c

        lax.fori_loop(0, chunks, both, 0)
        return c

    lax.fori_loop(1, n, settle_ctx, 0)
    filt_out[...] = gfr[...]

    def settle_ch(i, c):
        pk_copy(row_me, lax.rem(row_me + m - i, m)).wait_recv()
        pk_copy(lax.rem(row_me + i, m), row_me).wait_send()
        return c

    lax.fori_loop(1, m, settle_ch, 0)
    peak_out[...] = jnp.max(pks[...], axis=0)


def scale_kernel(prod, peak, filt, oq, ok, ov, of, op, done, small, sems, small_sems):
    channels, rows = prod.shape[1:]
    blocks = small.shape[0]
    per = rows // blocks
    outs = (oq, ok, ov)
    filt_copy = pltpu.make_async_copy(filt, of, small_sems.at[0])
    filt_copy.start()
    inv = 1.0 / (peak[0:3, :] + EPS)
    step = min(256, channels)

    def out_copy(i, r):
        at = pl.ds(r * step, step)
        return pltpu.make_async_copy(done.at[i, at, :], outs[i].at[at, :], sems.at[i, r])

    for r in range(channels // step):
        for i in range(3):
            at = pl.ds(r * step, step)
            done[i, at, :] = (prod[i, at, :] * inv[i : i + 1]).astype(jnp.bfloat16)
            out_copy(i, r).start()
    at_block = lax.broadcasted_iota(jnp.int32, (blocks, 3), 0)
    at_kind = lax.broadcasted_iota(jnp.int32, (blocks, 3), 1)
    table = jnp.zeros((blocks, 3), jnp.float32)
    for b in range(blocks):
        for i in range(3):
            table = jnp.where(
                (at_block == b) & (at_kind == i), peak[i : i + 1, b * per : b * per + 1], table
            )
    small[...] = table
    peak_copy = pltpu.make_async_copy(small, op, small_sems.at[1])
    peak_copy.start()
    for r in range(channels // step):
        for i in range(3):
            out_copy(i, r).wait()
    filt_copy.wait()
    peak_copy.wait()


def shards(n, m, q_vals, k_vals, v_vals, grad_out, exponents, filter_taps):
    channels, rows = q_vals.shape
    groups, filter_len = filter_taps.shape
    _, scale_blocks, blocks = exponents.shape
    scale_rows = channels // scale_blocks
    group_width = channels // groups
    own = channels // n
    own_groups = groups // n
    chunks = min(MOST_CHUNKS, own_groups)
    cols = filter_len // n
    lead = filter_len // rows
    bf16, f32 = jnp.bfloat16, jnp.float32
    anywhere = pl.BlockSpec(memory_space=pl.ANY)
    vmem = pl.BlockSpec(memory_space=pltpu.VMEM)
    dma = pltpu.SemaphoreType.DMA
    prod, filt, peak = pl.pallas_call(
        functools.partial(exchange_kernel, n, m, chunks, group_width, scale_rows, scale_blocks, blocks),
        out_shape=(
            jax.ShapeDtypeStruct((3, channels, rows), f32),
            jax.ShapeDtypeStruct((n, own_groups, cols), f32),
            jax.ShapeDtypeStruct((8, rows), f32),
        ),
        in_specs=[pl.BlockSpec(memory_space=pltpu.HBM)] * 6,
        out_specs=(vmem, vmem, vmem),
        scratch_shapes=[
            *[pltpu.VMEM((n, own, rows), bf16) for _ in range(4)],
            pltpu.VMEM((3, blocks, scale_blocks), jnp.int32),
            pltpu.VMEM((own_groups, filter_len), f32),
            pltpu.VMEM((3 * scale_blocks, 1, rows), f32),
            pltpu.VMEM((2, channels, rows), bf16),
            pltpu.VMEM((n, 2, own, rows), bf16),
            pltpu.VMEM((n, 2, own, rows), bf16),
            pltpu.VMEM((2, channels, rows), bf16),
            pltpu.VMEM(((lead + 1) * rows, rows), bf16),
            pltpu.VMEM(((lead + 1) * rows, rows), bf16),
            pltpu.VMEM((n, own_groups, cols), f32),
            pltpu.VMEM((n, own_groups, cols), f32),
            pltpu.VMEM((3, 8, rows), f32),
            pltpu.VMEM((m, 8, rows), f32),
            dma((4, chunks)),
            dma((2,)),
            dma((chunks, n)),
            dma((chunks, n)),
            dma((chunks, n)),
            dma((chunks, n)),
            dma((n,)),
            dma((n,)),
            dma((m,)),
            dma((m,)),
        ],
        compiler_params=pltpu.CompilerParams(
            collective_id=0, has_side_effects=True, vmem_limit_bytes=32 * 1024 * 1024
        ),
    )(
        *[
            pltpu.with_memory_space_constraint(x, pltpu.HBM)
            for x in (
                *[x.reshape(n, own, rows) for x in (q_vals, k_vals, v_vals, grad_out)],
                exponents.transpose(0, 2, 1),
                filter_taps.reshape(n, own_groups, filter_len),
            )
        ]
    )
    flat = jax.ShapeDtypeStruct((channels, rows), bf16)
    *grads, filt, peak = pl.pallas_call(
        scale_kernel,
        out_shape=(
            flat, flat, flat,
            jax.ShapeDtypeStruct((n, own_groups, cols), f32),
            jax.ShapeDtypeStruct((blocks, 3), f32),
        ),
        in_specs=[vmem] * 3,
        out_specs=[anywhere] * 5,
        scratch_shapes=[
            pltpu.VMEM((3, channels, rows), bf16),
            pltpu.VMEM((blocks, 3), f32),
            dma((3, channels // min(256, channels))),
            dma((2,)),
        ],
        compiler_params=pltpu.CompilerParams(vmem_limit_bytes=16 * 1024 * 1024),
    )(prod, peak, filt)
    return (*grads, filt.reshape(groups, cols), peak.T)


def solution(mesh):
    in_specs = (
        P("ch", "ctx"),
        P("ch", "ctx"),
        P("ch", "ctx"),
        P("ch", "ctx"),
        P(None, "ch", "ctx"),
        P("ch", None),
    )
    out_specs = (P("ch", "ctx"), P("ch", "ctx"), P("ch", "ctx"), P("ch", "ctx"), P(None, "ctx"))
    body = functools.partial(shards, mesh.shape["ctx"], mesh.shape["ch"])
    return jax.shard_map(body, mesh=mesh, in_specs=in_specs, out_specs=out_specs, check_vma=False)
```

```python
import functools

import jax
import jax.numpy as jnp
from jax import lax
from jax.experimental import pallas as pl
from jax.experimental.pallas import tpu as pltpu
from jax.sharding import PartitionSpec as P

EPS = 1e-06
MESH = pl.DeviceIdType.MESH
MOST_CHUNKS = 8
HALF = 128


def exchange_kernel(
    n, m, chunks, group_width, scale_rows, scale_blocks, blocks,
    q_in, k_in, v_in, g_in, ex_in, taps_in,
    prod_out, filt_out, peak_out,
    q_ref, k_ref, v_ref, g_ref, ex_ref, taps_ref, sc_ref,
    zs, zf, ws, wr, tt0, tt1, gfs, gfr, peak, pks,
    load_sem, small_sem,
    in_send, in_recv, back_send, back_recv, gf_send, gf_recv, pk_send, pk_recv,
):
    me = lax.axis_index("ctx")
    row_me = lax.axis_index("ch")
    _, own, rows = q_ref.shape
    chunk = own // chunks
    own_groups = own // group_width
    chunk_groups = own_groups // chunks
    filter_len = taps_ref.shape[1]
    lead = filter_len // rows
    cols = filter_len // n
    width = filter_len + HALF
    f32 = jnp.float32
    chips = n // 2

    def flipped(mask):
        out, bit = 0, 1
        while bit < n:
            out = out + lax.rem(lax.div(me, bit) + lax.div(mask, bit), 2) * bit
            bit *= 2
        return out

    core = lax.rem(me, 2)
    peers = []
    for low in range(2):
        for h in range(1, chips):
            swap = (1 if h == 1 else -1 if h == 2 else 0) if chips > 2 else 0
            peers.append(flipped((h + core * swap) * 2 + low))
    peers.append(flipped(jnp.int32(1)))

    loads = tuple(zip((k_in, v_in, q_in, g_in), (k_ref, v_ref, q_ref, g_ref)))

    def load_copy(i, j):
        part = pl.ds(pl.multiple_of(j * chunk, 16), chunk)
        src, dst = loads[i]
        return pltpu.make_async_copy(src.at[:, part, :], dst.at[:, part, :], load_sem.at[i, j])

    ex_copy = pltpu.make_async_copy(ex_in, ex_ref, small_sem.at[0])
    taps_copy = pltpu.make_async_copy(taps_in.at[me], taps_ref, small_sem.at[1])
    ex_copy.start()

    def load_chunk(j, c):
        for i in range(4):
            load_copy(i, j).start()
        return c

    barrier = pltpu.get_barrier_semaphore()

    def greet_ctx(i, c):
        pl.semaphore_signal(
            barrier, inc=1, device_id={"ctx": lax.rem(me + i, n)}, device_id_type=MESH
        )
        return c

    def greet_ch(i, c):
        pl.semaphore_signal(
            barrier, inc=1, device_id={"ch": lax.rem(row_me + i, m)}, device_id_type=MESH
        )
        return c

    lax.fori_loop(1, n, greet_ctx, 0)
    lax.fori_loop(1, m, greet_ch, 0)
    lax.fori_loop(0, chunks, load_chunk, 0)
    taps_copy.start()
    ex_copy.wait()
    per_scale = rows // blocks
    for a in range(3):
        scale = jnp.exp2(ex_ref[a].astype(f32))
        for i in range(scale_blocks):
            sc_ref[a * scale_blocks + i] = jnp.concatenate(
                [jnp.broadcast_to(scale[b : b + 1, i : i + 1], (1, per_scale)) for b in range(blocks)], axis=1
            )

    def at_rows(owner, j):
        return pl.ds(pl.multiple_of(owner * own + j * chunk, 16), chunk)

    def at_part(j):
        return pl.ds(pl.multiple_of(j * chunk, 16), chunk)

    def scale_of(which, owner, j):
        return sc_ref[which * scale_blocks + (owner * own + j * chunk) // scale_rows]

    def real(ref, which, owner, j):
        return ref[owner, at_part(j), :].astype(f32) * scale_of(which, owner, j)

    def mixed(owner, j):
        z = (real(k_ref, 1, owner, j) * real(v_ref, 2, owner, j)).astype(jnp.bfloat16)
        gw = (real(q_ref, 0, owner, j) * g_ref[owner, at_part(j), :].astype(f32)).astype(jnp.bfloat16)
        return z, gw

    def in_copy(j, dst, src):
        return pltpu.make_async_remote_copy(
            src_ref=zs.at[:, at_rows(dst, j), :],
            dst_ref=zf.at[src, :, pl.ds(pl.multiple_of(j * chunk, 16), chunk), :],
            send_sem=in_send.at[j, dst],
            recv_sem=in_recv.at[j, src],
            device_id={"ctx": dst},
            device_id_type=MESH,
        )

    def back_copy(j, dst, src):
        return pltpu.make_async_remote_copy(
            src_ref=ws.at[dst, :, pl.ds(pl.multiple_of(j * chunk, 16), chunk), :],
            dst_ref=wr.at[:, at_rows(src, j), :],
            send_sem=back_send.at[j, dst],
            recv_sem=back_recv.at[j, src],
            device_id={"ctx": dst},
            device_id_type=MESH,
        )

    def gf_copy(dst, src):
        return pltpu.make_async_remote_copy(
            src_ref=gfs.at[dst],
            dst_ref=gfr.at[src],
            send_sem=gf_send.at[dst],
            recv_sem=gf_recv.at[src],
            device_id={"ctx": dst},
            device_id_type=MESH,
        )

    def pk_copy(dst, src):
        return pltpu.make_async_remote_copy(
            src_ref=pks.at[row_me],
            dst_ref=pks.at[src],
            send_sem=pk_send.at[dst],
            recv_sem=pk_recv.at[src],
            device_id={"ch": dst},
            device_id_type=MESH,
        )

    pl.semaphore_wait(barrier, n - 1 + m - 1)

    def send_chunk(j, c):
        for i in range(4):
            load_copy(i, j).wait()

        for dst in peers:
            z, gw = mixed(dst, j)
            zs[0, at_rows(dst, j), :] = z
            zs[1, at_rows(dst, j), :] = gw
            in_copy(j, dst, me).start()
        z, gw = mixed(me, j)
        here = pl.ds(pl.multiple_of(j * chunk, 16), chunk)
        zf[me, 0, here, :] = z
        zf[me, 1, here, :] = gw
        return c

    lax.fori_loop(0, chunks, send_chunk, 0)

    taps_copy.wait()
    peak[...] = jnp.zeros_like(peak)
    flip = (
        lax.broadcasted_iota(jnp.int32, (HALF, HALF), 0)
        + lax.broadcasted_iota(jnp.int32, (HALF, HALF), 1)
        == HALF - 1
    ).astype(f32).astype(jnp.bfloat16)
    zero = jnp.zeros((HALF, HALF), jnp.bfloat16)

    def turned(x, by):
        by = (by * group_width) % x.shape[0]
        return x if by == 0 else jnp.concatenate([x[-by:], x[:-by]], axis=0)

    def one_group(gi, tt):
        at = pl.ds(pl.multiple_of(gi * group_width, 16), group_width)
        z = zf[:, 0, at, :].reshape(n * group_width, rows)
        gw = zf[:, 1, at, :].reshape(n * group_width, rows)
        taps = taps_ref[pl.ds(gi, 1), :].astype(jnp.bfloat16).astype(f32)
        line = jnp.concatenate([taps, jnp.zeros((1, HALF), f32)], axis=1)
        band = pltpu.roll(
            jnp.broadcast_to(line, (HALF, width)), 0, 1, stride=1, stride_axis=0
        ).astype(jnp.bfloat16)

        def tile(i):
            if i < 0 or i * HALF >= width:
                return zero
            return band[:, i * HALF : (i + 1) * HALF]

        per = rows // HALF
        for o in range(lead + 1):
            for a in range(per):
                for b in range(per):
                    tt[o * rows + a * HALF : o * rows + (a + 1) * HALF, b * HALF : (b + 1) * HALF] = tile(
                        o * per + b - a
                    )
        zwin = jnp.concatenate([turned(z, o) for o in range(lead + 1)], axis=1)
        w = jnp.dot(zwin, tt[...], preferred_element_type=f32)
        gparts = [turned(gw, -o) for o in range(lead + 1)]
        gz = jnp.zeros((n * group_width, rows), f32)
        for o in range(lead + 1):
            gz = gz + lax.dot_general(
                gparts[o], tt[o * rows : (o + 1) * rows, :], (((1,), (1,)), ((), ())),
                preferred_element_type=f32,
            )
        ws[:, 0, at, :] = w.astype(jnp.bfloat16).reshape(n, group_width, rows)
        ws[:, 1, at, :] = gz.astype(jnp.bfloat16).reshape(n, group_width, rows)

        gwin = jnp.concatenate(gparts, axis=1)
        zcat = jnp.concatenate([z[:, a * HALF : (a + 1) * HALF] for a in range(per)], axis=0)
        gcat = jnp.concatenate([gwin[:, a * HALF : a * HALF + width] for a in range(per)], axis=0)
        zrev = lax.dot_general(
            flip, zcat, (((1,), (1,)), ((), ())), preferred_element_type=f32
        ).astype(jnp.bfloat16)
        cross = jnp.dot(zrev, gcat, preferred_element_type=f32)
        skewed = pltpu.roll(cross, width - (HALF - 1), 1, stride=1, stride_axis=0)
        lags = jnp.sum(skewed, axis=0, keepdims=True)
        for d in range(n):
            gfs[d, pl.ds(gi, 1), :] = lags[:, d * cols : (d + 1) * cols]

    def note_peak(j, owner):
        conv = wr[0, at_rows(owner, j), :].astype(f32)
        gz = wr[1, at_rows(owner, j), :].astype(f32)
        gq = g_ref[owner, at_part(j), :].astype(f32) * conv
        gk = gz * real(v_ref, 2, owner, j)
        gv = gz * real(k_ref, 1, owner, j)
        for i, x in enumerate((gq, gk, gv)):
            prod_out[i, at_rows(owner, j), :] = x
            peak[i] = jnp.maximum(peak[i], jnp.max(jnp.abs(x).reshape(chunk // 8, 8, rows), axis=0))

    def take_back(j):
        for src in peers:
            back_copy(j, me, src).wait_recv()
            note_peak(j, src)
        note_peak(j, me)

    def work_chunk(j, c):
        for src in peers:
            in_copy(j, me, src).wait_recv()
        for u in range(chunk_groups):
            one_group(j * chunk_groups + u, tt1 if u % 2 else tt0)

        for dst in peers:
            back_copy(j, dst, me).start()
        here = pl.ds(pl.multiple_of(j * chunk, 16), chunk)
        for i in range(2):
            wr[i, at_rows(me, j), :] = ws[me, i, here, :]
        return c

    lax.fori_loop(0, chunks, work_chunk, 0)

    def send_gf(i, c):
        gf_copy(lax.rem(me + i, n), me).start()
        return c

    lax.fori_loop(1, n, send_gf, 0)

    def take_chunk(j, c):
        take_back(j)
        return c

    lax.fori_loop(0, chunks, take_chunk, 0)

    for i in range(3):
        lanes = jnp.max(peak[i], axis=0, keepdims=True)
        per = rows // blocks
        pks[row_me, i : i + 1, :] = jnp.concatenate(
            [
                jnp.broadcast_to(jnp.max(lanes[:, b * per : (b + 1) * per], axis=1, keepdims=True), (1, per))
                for b in range(blocks)
            ],
            axis=1,
        )
    pks[row_me, 3:8, :] = jnp.zeros((5, rows), f32)

    def send_pk(i, c):
        pk_copy(lax.rem(row_me + i, m), row_me).start()
        return c

    lax.fori_loop(1, m, send_pk, 0)

    gfr[me] = gfs[me]

    def settle_ctx(i, c):
        dst = lax.rem(me + i, n)
        src = lax.rem(me + n - i, n)
        gf_copy(me, src).wait_recv()
        gf_copy(dst, me).wait_send()

        def both(j, c):
            in_copy(j, dst, me).wait_send()
            back_copy(j, dst, me).wait_send()
            return c

        lax.fori_loop(0, chunks, both, 0)
        return c

    lax.fori_loop(1, n, settle_ctx, 0)
    filt_out[...] = gfr[...]

    def settle_ch(i, c):
        pk_copy(row_me, lax.rem(row_me + m - i, m)).wait_recv()
        pk_copy(lax.rem(row_me + i, m), row_me).wait_send()
        return c

    lax.fori_loop(1, m, settle_ch, 0)
    peak_out[...] = jnp.max(pks[...], axis=0)


def scale_kernel(prod, peak, filt, oq, ok, ov, of, op, done, small, sems, small_sems):
    channels, rows = prod.shape[1:]
    blocks = small.shape[0]
    per = rows // blocks
    outs = (oq, ok, ov)
    filt_copy = pltpu.make_async_copy(filt, of, small_sems.at[0])
    filt_copy.start()
    inv = 1.0 / (peak[0:3, :] + EPS)
    step = min(256, channels)

    def out_copy(i, r):
        at = pl.ds(r * step, step)
        return pltpu.make_async_copy(done.at[i, at, :], outs[i].at[at, :], sems.at[i, r])

    for r in range(channels // step):
        for i in range(3):
            at = pl.ds(r * step, step)
            done[i, at, :] = (prod[i, at, :] * inv[i : i + 1]).astype(jnp.bfloat16)
            out_copy(i, r).start()
    at_block = lax.broadcasted_iota(jnp.int32, (blocks, 3), 0)
    at_kind = lax.broadcasted_iota(jnp.int32, (blocks, 3), 1)
    table = jnp.zeros((blocks, 3), jnp.float32)
    for b in range(blocks):
        for i in range(3):
            table = jnp.where(
                (at_block == b) & (at_kind == i), peak[i : i + 1, b * per : b * per + 1], table
            )
    small[...] = table
    peak_copy = pltpu.make_async_copy(small, op, small_sems.at[1])
    peak_copy.start()
    for r in range(channels // step):
        for i in range(3):
            out_copy(i, r).wait()
    filt_copy.wait()
    peak_copy.wait()


def shards(n, m, q_vals, k_vals, v_vals, grad_out, exponents, filter_taps):
    channels, rows = q_vals.shape
    groups, filter_len = filter_taps.shape
    _, scale_blocks, blocks = exponents.shape
    scale_rows = channels // scale_blocks
    group_width = channels // groups
    own = channels // n
    own_groups = groups // n
    chunks = min(MOST_CHUNKS, own_groups)
    cols = filter_len // n
    lead = filter_len // rows
    bf16, f32 = jnp.bfloat16, jnp.float32
    anywhere = pl.BlockSpec(memory_space=pl.ANY)
    vmem = pl.BlockSpec(memory_space=pltpu.VMEM)
    dma = pltpu.SemaphoreType.DMA
    prod, filt, peak = pl.pallas_call(
        functools.partial(exchange_kernel, n, m, chunks, group_width, scale_rows, scale_blocks, blocks),
        out_shape=(
            jax.ShapeDtypeStruct((3, channels, rows), f32),
            jax.ShapeDtypeStruct((n, own_groups, cols), f32),
            jax.ShapeDtypeStruct((8, rows), f32),
        ),
        in_specs=[pl.BlockSpec(memory_space=pltpu.HBM)] * 6,
        out_specs=(vmem, vmem, vmem),
        scratch_shapes=[
            *[pltpu.VMEM((n, own, rows), bf16) for _ in range(4)],
            pltpu.VMEM((3, blocks, scale_blocks), jnp.int32),
            pltpu.VMEM((own_groups, filter_len), f32),
            pltpu.VMEM((3 * scale_blocks, 1, rows), f32),
            pltpu.VMEM((2, channels, rows), bf16),
            pltpu.VMEM((n, 2, own, rows), bf16),
            pltpu.VMEM((n, 2, own, rows), bf16),
            pltpu.VMEM((2, channels, rows), bf16),
            pltpu.VMEM(((lead + 1) * rows, rows), bf16),
            pltpu.VMEM(((lead + 1) * rows, rows), bf16),
            pltpu.VMEM((n, own_groups, cols), f32),
            pltpu.VMEM((n, own_groups, cols), f32),
            pltpu.VMEM((3, 8, rows), f32),
            pltpu.VMEM((m, 8, rows), f32),
            dma((4, chunks)),
            dma((2,)),
            dma((chunks, n)),
            dma((chunks, n)),
            dma((chunks, n)),
            dma((chunks, n)),
            dma((n,)),
            dma((n,)),
            dma((m,)),
            dma((m,)),
        ],
        compiler_params=pltpu.CompilerParams(
            collective_id=0, has_side_effects=True, vmem_limit_bytes=32 * 1024 * 1024
        ),
    )(
        *[
            pltpu.with_memory_space_constraint(x, pltpu.HBM)
            for x in (
                *[x.reshape(n, own, rows) for x in (q_vals, k_vals, v_vals, grad_out)],
                exponents.transpose(0, 2, 1),
                filter_taps.reshape(n, own_groups, filter_len),
            )
        ]
    )
    flat = jax.ShapeDtypeStruct((channels, rows), bf16)
    *grads, filt, peak = pl.pallas_call(
        scale_kernel,
        out_shape=(
            flat, flat, flat,
            jax.ShapeDtypeStruct((n, own_groups, cols), f32),
            jax.ShapeDtypeStruct((blocks, 3), f32),
        ),
        in_specs=[vmem] * 3,
        out_specs=[anywhere] * 5,
        scratch_shapes=[
            pltpu.VMEM((3, channels, rows), bf16),
            pltpu.VMEM((blocks, 3), f32),
            dma((3, channels // min(256, channels))),
            dma((2,)),
        ],
        compiler_params=pltpu.CompilerParams(vmem_limit_bytes=16 * 1024 * 1024),
    )(prod, peak, filt)
    return (*grads, filt.reshape(groups, cols), peak.T)


def solution(mesh):
    in_specs = (
        P("ch", "ctx"),
        P("ch", "ctx"),
        P("ch", "ctx"),
        P("ch", "ctx"),
        P(None, "ch", "ctx"),
        P("ch", None),
    )
    out_specs = (P("ch", "ctx"), P("ch", "ctx"), P("ch", "ctx"), P("ch", "ctx"), P(None, "ctx"))
    body = functools.partial(shards, mesh.shape["ctx"], mesh.shape["ch"])
    return jax.shard_map(body, mesh=mesh, in_specs=in_specs, out_specs=out_specs, check_vma=False)
```

```python
import functools

import jax
import jax.numpy as jnp
from jax import lax
from jax.experimental import pallas as pl
from jax.experimental.pallas import tpu as pltpu
from jax.sharding import PartitionSpec as P

EPS = 1e-06
MESH = pl.DeviceIdType.MESH
MOST_CHUNKS = 8
HALF = 128


def exchange_kernel(
    n, m, chunks, group_width, scale_rows, scale_blocks, blocks,
    q_in, k_in, v_in, g_in, ex_in, taps_in,
    prod_out, filt_out, peak_out,
    q_ref, k_ref, v_ref, g_ref, ex_ref, taps_ref, sc_ref,
    zs, zf, ws, wr, tt0, tt1, flip_ref, lags, gfs, gfr, peak, pks,
    load_sem, small_sem,
    in_send, in_recv, back_send, back_recv, gf_send, gf_recv, pk_send, pk_recv,
):
    me = lax.axis_index("ctx")
    row_me = lax.axis_index("ch")
    _, own, rows = q_ref.shape
    chunk = own // chunks
    own_groups = own // group_width
    chunk_groups = own_groups // chunks
    filter_len = taps_ref.shape[1]
    lead = filter_len // rows
    cols = filter_len // n
    width = filter_len + HALF
    f32 = jnp.float32
    chips = n // 2

    def flipped(mask):
        out, bit = 0, 1
        while bit < n:
            out = out + lax.rem(lax.div(me, bit) + lax.div(mask, bit), 2) * bit
            bit *= 2
        return out

    core = lax.rem(me, 2)
    peers = []
    for low in range(2):
        for h in range(1, chips):
            swap = (1 if h == 1 else -1 if h == 2 else 0) if chips > 2 else 0
            peers.append(flipped((h + core * swap) * 2 + low))
    peers.append(flipped(jnp.int32(1)))

    loads = tuple(zip((k_in, v_in, q_in, g_in), (k_ref, v_ref, q_ref, g_ref)))

    def load_copy(i, j):
        part = pl.ds(pl.multiple_of(j * chunk, 16), chunk)
        src, dst = loads[i]
        return pltpu.make_async_copy(src.at[:, part, :], dst.at[:, part, :], load_sem.at[i, j])

    ex_copy = pltpu.make_async_copy(ex_in, ex_ref, small_sem.at[0])
    taps_copy = pltpu.make_async_copy(taps_in.at[me], taps_ref, small_sem.at[1])
    ex_copy.start()

    def load_chunk(j, c):
        for i in range(4):
            load_copy(i, j).start()
        return c

    barrier = pltpu.get_barrier_semaphore()

    def greet_ctx(i, c):
        pl.semaphore_signal(
            barrier, inc=1, device_id={"ctx": lax.rem(me + i, n)}, device_id_type=MESH
        )
        return c

    def greet_ch(i, c):
        pl.semaphore_signal(
            barrier, inc=1, device_id={"ch": lax.rem(row_me + i, m)}, device_id_type=MESH
        )
        return c

    lax.fori_loop(1, n, greet_ctx, 0)
    lax.fori_loop(1, m, greet_ch, 0)
    lax.fori_loop(0, chunks, load_chunk, 0)
    taps_copy.start()
    ex_copy.wait()
    per_scale = rows // blocks
    for a in range(3):
        scale = jnp.exp2(ex_ref[a].astype(f32))
        for i in range(scale_blocks):
            sc_ref[a * scale_blocks + i] = jnp.concatenate(
                [jnp.broadcast_to(scale[b : b + 1, i : i + 1], (1, per_scale)) for b in range(blocks)], axis=1
            )

    def at_rows(owner, j):
        return pl.ds(pl.multiple_of(owner * own + j * chunk, 16), chunk)

    def at_part(j):
        return pl.ds(pl.multiple_of(j * chunk, 16), chunk)

    def scale_of(which, owner, j):
        return sc_ref[which * scale_blocks + (owner * own + j * chunk) // scale_rows]

    def real(ref, which, owner, j):
        return ref[owner, at_part(j), :].astype(f32) * scale_of(which, owner, j)

    def mixed(owner, j):
        z = (real(k_ref, 1, owner, j) * real(v_ref, 2, owner, j)).astype(jnp.bfloat16)
        gw = (real(q_ref, 0, owner, j) * g_ref[owner, at_part(j), :].astype(f32)).astype(jnp.bfloat16)
        return z, gw

    def in_copy(j, dst, src):
        return pltpu.make_async_remote_copy(
            src_ref=zs.at[:, at_rows(dst, j), :],
            dst_ref=zf.at[src, :, pl.ds(pl.multiple_of(j * chunk, 16), chunk), :],
            send_sem=in_send.at[j, dst],
            recv_sem=in_recv.at[j, src],
            device_id={"ctx": dst},
            device_id_type=MESH,
        )

    def back_copy(j, dst, src):
        return pltpu.make_async_remote_copy(
            src_ref=ws.at[dst, :, pl.ds(pl.multiple_of(j * chunk, 16), chunk), :],
            dst_ref=wr.at[:, at_rows(src, j), :],
            send_sem=back_send.at[j, dst],
            recv_sem=back_recv.at[j, src],
            device_id={"ctx": dst},
            device_id_type=MESH,
        )

    def gf_copy(dst, src):
        return pltpu.make_async_remote_copy(
            src_ref=gfs.at[dst],
            dst_ref=gfr.at[src],
            send_sem=gf_send.at[dst],
            recv_sem=gf_recv.at[src],
            device_id={"ctx": dst},
            device_id_type=MESH,
        )

    def pk_copy(dst, src):
        return pltpu.make_async_remote_copy(
            src_ref=pks.at[row_me],
            dst_ref=pks.at[src],
            send_sem=pk_send.at[dst],
            recv_sem=pk_recv.at[src],
            device_id={"ch": dst},
            device_id_type=MESH,
        )

    pl.semaphore_wait(barrier, n - 1 + m - 1)

    def send_chunk(j, c):
        for i in range(4):
            load_copy(i, j).wait()

        for dst in peers:
            z, gw = mixed(dst, j)
            zs[0, at_rows(dst, j), :] = z
            zs[1, at_rows(dst, j), :] = gw
            in_copy(j, dst, me).start()
        z, gw = mixed(me, j)
        here = pl.ds(pl.multiple_of(j * chunk, 16), chunk)
        zf[me, 0, here, :] = z
        zf[me, 1, here, :] = gw
        return c

    lax.fori_loop(0, chunks, send_chunk, 0)

    taps_copy.wait()
    peak[...] = jnp.zeros_like(peak)
    def mirror(size, kind):
        at = lax.broadcasted_iota(jnp.int32, (size, size), 0)
        to = lax.broadcasted_iota(jnp.int32, (size, size), 1)
        return (at + to == size - 1).astype(f32).astype(kind)

    flip_ref[...] = mirror(rows, jnp.bfloat16)
    zero = jnp.zeros((HALF, HALF), jnp.bfloat16)

    def turned(x, by):
        by = (by * group_width) % x.shape[0]
        return x if by == 0 else jnp.concatenate([x[-by:], x[:-by]], axis=0)

    def one_group(gi, tt):
        at = pl.ds(pl.multiple_of(gi * group_width, 16), group_width)
        z = zf[:, 0, at, :].reshape(n * group_width, rows)
        gw = zf[:, 1, at, :].reshape(n * group_width, rows)
        taps = taps_ref[pl.ds(gi, 1), :].astype(jnp.bfloat16).astype(f32)
        line = jnp.concatenate([taps, jnp.zeros((1, HALF), f32)], axis=1)
        band = pltpu.roll(
            jnp.broadcast_to(line, (HALF, width)), 0, 1, stride=1, stride_axis=0
        ).astype(jnp.bfloat16)

        def tile(i):
            if i < 0 or i * HALF >= width:
                return zero
            return band[:, i * HALF : (i + 1) * HALF]

        per = rows // HALF
        for o in range(lead + 1):
            for a in range(per):
                for b in range(per):
                    tt[o * rows + a * HALF : o * rows + (a + 1) * HALF, b * HALF : (b + 1) * HALF] = tile(
                        o * per + b - a
                    )
        gw = jnp.dot(gw, flip_ref[...], preferred_element_type=f32).astype(jnp.bfloat16)
        gparts = [turned(gw, -o) for o in range(lead + 1)]
        both = jnp.concatenate(
            [
                jnp.concatenate([turned(z, o) for o in range(lead + 1)], axis=1),
                jnp.concatenate(gparts, axis=1),
            ],
            axis=0,
        )
        res = jnp.dot(both, tt[...], preferred_element_type=f32).astype(jnp.bfloat16)
        w = res[: n * group_width]
        gz = jnp.dot(res[n * group_width :], flip_ref[...], preferred_element_type=f32)
        ws[:, 0, at, :] = w.reshape(n, group_width, rows)
        ws[:, 1, at, :] = gz.astype(jnp.bfloat16).reshape(n, group_width, rows)

        gwin = jnp.concatenate(gparts[::-1], axis=1)
        zcat = jnp.concatenate([z[:, a * HALF : (a + 1) * HALF] for a in range(per)], axis=0)
        gcat = jnp.concatenate(
            [gwin[:, (per - 1 - a) * HALF : (per - 1 - a) * HALF + width] for a in range(per)], axis=0
        )
        cross = lax.dot_general(zcat, gcat, (((0,), (0,)), ((), ())), preferred_element_type=f32)
        skewed = pltpu.roll(cross, 0, 1, stride=1, stride_axis=0)
        lags[pl.ds(gi, 1), :] = jnp.sum(skewed, axis=0, keepdims=True)[:, HALF:]

    def note_peak(j, owner):
        conv = wr[0, at_rows(owner, j), :].astype(f32)
        gz = wr[1, at_rows(owner, j), :].astype(f32)
        gq = g_ref[owner, at_part(j), :].astype(f32) * conv
        gk = gz * real(v_ref, 2, owner, j)
        gv = gz * real(k_ref, 1, owner, j)
        for i, x in enumerate((gq, gk, gv)):
            prod_out[i, at_rows(owner, j), :] = x
            peak[i] = jnp.maximum(peak[i], jnp.max(jnp.abs(x).reshape(chunk // 8, 8, rows), axis=0))

    def take_back(j):
        for src in peers:
            back_copy(j, me, src).wait_recv()
            note_peak(j, src)
        note_peak(j, me)

    def work_chunk(j, c):
        for src in peers:
            in_copy(j, me, src).wait_recv()
        for u in range(chunk_groups):
            one_group(j * chunk_groups + u, tt1 if u % 2 else tt0)

        for dst in peers:
            back_copy(j, dst, me).start()
        here = pl.ds(pl.multiple_of(j * chunk, 16), chunk)
        for i in range(2):
            wr[i, at_rows(me, j), :] = ws[me, i, here, :]
        return c

    lax.fori_loop(0, chunks, work_chunk, 0)

    back = mirror(HALF, f32)
    straight = jnp.concatenate(
        [
            jnp.dot(
                lags[:, i : i + HALF], back, preferred_element_type=f32, precision=lax.Precision.HIGHEST
            )
            for i in range(filter_len - HALF, -1, -HALF)
        ],
        axis=1,
    )
    for d in range(n):
        gfs[d] = straight[:, d * cols : (d + 1) * cols]

    def send_gf(i, c):
        gf_copy(lax.rem(me + i, n), me).start()
        return c

    lax.fori_loop(1, n, send_gf, 0)

    def take_chunk(j, c):
        take_back(j)
        return c

    lax.fori_loop(0, chunks, take_chunk, 0)

    for i in range(3):
        lanes = jnp.max(peak[i], axis=0, keepdims=True)
        per = rows // blocks
        pks[row_me, i : i + 1, :] = jnp.concatenate(
            [
                jnp.broadcast_to(jnp.max(lanes[:, b * per : (b + 1) * per], axis=1, keepdims=True), (1, per))
                for b in range(blocks)
            ],
            axis=1,
        )
    pks[row_me, 3:8, :] = jnp.zeros((5, rows), f32)

    def send_pk(i, c):
        pk_copy(lax.rem(row_me + i, m), row_me).start()
        return c

    lax.fori_loop(1, m, send_pk, 0)

    gfr[me] = gfs[me]

    def settle_ctx(i, c):
        dst = lax.rem(me + i, n)
        src = lax.rem(me + n - i, n)
        gf_copy(me, src).wait_recv()
        gf_copy(dst, me).wait_send()

        def both(j, c):
            in_copy(j, dst, me).wait_send()
            back_copy(j, dst, me).wait_send()
            return c

        lax.fori_loop(0, chunks, both, 0)
        return c

    lax.fori_loop(1, n, settle_ctx, 0)
    filt_out[...] = gfr[...]

    def settle_ch(i, c):
        pk_copy(row_me, lax.rem(row_me + m - i, m)).wait_recv()
        pk_copy(lax.rem(row_me + i, m), row_me).wait_send()
        return c

    lax.fori_loop(1, m, settle_ch, 0)
    peak_out[...] = jnp.max(pks[...], axis=0)


def scale_kernel(prod, peak, filt, oq, ok, ov, of, op, done, small, sems, small_sems):
    channels, rows = prod.shape[1:]
    blocks = small.shape[0]
    per = rows // blocks
    outs = (oq, ok, ov)
    filt_copy = pltpu.make_async_copy(filt, of, small_sems.at[0])
    filt_copy.start()
    inv = 1.0 / (peak[0:3, :] + EPS)
    step = min(256, channels)

    def out_copy(i, r):
        at = pl.ds(r * step, step)
        return pltpu.make_async_copy(done.at[i, at, :], outs[i].at[at, :], sems.at[i, r])

    for r in range(channels // step):
        for i in range(3):
            at = pl.ds(r * step, step)
            done[i, at, :] = (prod[i, at, :] * inv[i : i + 1]).astype(jnp.bfloat16)
            out_copy(i, r).start()
    at_block = lax.broadcasted_iota(jnp.int32, (blocks, 3), 0)
    at_kind = lax.broadcasted_iota(jnp.int32, (blocks, 3), 1)
    table = jnp.zeros((blocks, 3), jnp.float32)
    for b in range(blocks):
        for i in range(3):
            table = jnp.where(
                (at_block == b) & (at_kind == i), peak[i : i + 1, b * per : b * per + 1], table
            )
    small[...] = table
    peak_copy = pltpu.make_async_copy(small, op, small_sems.at[1])
    peak_copy.start()
    for r in range(channels // step):
        for i in range(3):
            out_copy(i, r).wait()
    filt_copy.wait()
    peak_copy.wait()


def shards(n, m, q_vals, k_vals, v_vals, grad_out, exponents, filter_taps):
    channels, rows = q_vals.shape
    groups, filter_len = filter_taps.shape
    _, scale_blocks, blocks = exponents.shape
    scale_rows = channels // scale_blocks
    group_width = channels // groups
    own = channels // n
    own_groups = groups // n
    chunks = min(MOST_CHUNKS, own_groups)
    cols = filter_len // n
    lead = filter_len // rows
    bf16, f32 = jnp.bfloat16, jnp.float32
    anywhere = pl.BlockSpec(memory_space=pl.ANY)
    vmem = pl.BlockSpec(memory_space=pltpu.VMEM)
    dma = pltpu.SemaphoreType.DMA
    prod, filt, peak = pl.pallas_call(
        functools.partial(exchange_kernel, n, m, chunks, group_width, scale_rows, scale_blocks, blocks),
        out_shape=(
            jax.ShapeDtypeStruct((3, channels, rows), f32),
            jax.ShapeDtypeStruct((n, own_groups, cols), f32),
            jax.ShapeDtypeStruct((8, rows), f32),
        ),
        in_specs=[pl.BlockSpec(memory_space=pltpu.HBM)] * 6,
        out_specs=(vmem, vmem, vmem),
        scratch_shapes=[
            *[pltpu.VMEM((n, own, rows), bf16) for _ in range(4)],
            pltpu.VMEM((3, blocks, scale_blocks), jnp.int32),
            pltpu.VMEM((own_groups, filter_len), f32),
            pltpu.VMEM((3 * scale_blocks, 1, rows), f32),
            pltpu.VMEM((2, channels, rows), bf16),
            pltpu.VMEM((n, 2, own, rows), bf16),
            pltpu.VMEM((n, 2, own, rows), bf16),
            pltpu.VMEM((2, channels, rows), bf16),
            pltpu.VMEM(((lead + 1) * rows, rows), bf16),
            pltpu.VMEM(((lead + 1) * rows, rows), bf16),
            pltpu.VMEM((rows, rows), bf16),
            pltpu.VMEM((own_groups, filter_len), f32),
            pltpu.VMEM((n, own_groups, cols), f32),
            pltpu.VMEM((n, own_groups, cols), f32),
            pltpu.VMEM((3, 8, rows), f32),
            pltpu.VMEM((m, 8, rows), f32),
            dma((4, chunks)),
            dma((2,)),
            dma((chunks, n)),
            dma((chunks, n)),
            dma((chunks, n)),
            dma((chunks, n)),
            dma((n,)),
            dma((n,)),
            dma((m,)),
            dma((m,)),
        ],
        compiler_params=pltpu.CompilerParams(
            collective_id=0, has_side_effects=True, vmem_limit_bytes=32 * 1024 * 1024
        ),
    )(
        *[
            pltpu.with_memory_space_constraint(x, pltpu.HBM)
            for x in (
                *[x.reshape(n, own, rows) for x in (q_vals, k_vals, v_vals, grad_out)],
                exponents.transpose(0, 2, 1),
                filter_taps.reshape(n, own_groups, filter_len),
            )
        ]
    )
    flat = jax.ShapeDtypeStruct((channels, rows), bf16)
    *grads, filt, peak = pl.pallas_call(
        scale_kernel,
        out_shape=(
            flat, flat, flat,
            jax.ShapeDtypeStruct((n, own_groups, cols), f32),
            jax.ShapeDtypeStruct((blocks, 3), f32),
        ),
        in_specs=[vmem] * 3,
        out_specs=[anywhere] * 5,
        scratch_shapes=[
            pltpu.VMEM((3, channels, rows), bf16),
            pltpu.VMEM((blocks, 3), f32),
            dma((3, channels // min(256, channels))),
            dma((2,)),
        ],
        compiler_params=pltpu.CompilerParams(vmem_limit_bytes=16 * 1024 * 1024),
    )(prod, peak, filt)
    return (*grads, filt.reshape(groups, cols), peak.T)


def solution(mesh):
    in_specs = (
        P("ch", "ctx"),
        P("ch", "ctx"),
        P("ch", "ctx"),
        P("ch", "ctx"),
        P(None, "ch", "ctx"),
        P("ch", None),
    )
    out_specs = (P("ch", "ctx"), P("ch", "ctx"), P("ch", "ctx"), P("ch", "ctx"), P(None, "ctx"))
    body = functools.partial(shards, mesh.shape["ctx"], mesh.shape["ch"])
    return jax.shard_map(body, mesh=mesh, in_specs=in_specs, out_specs=out_specs, check_vma=False)
```

```python
import functools

import jax
import jax.numpy as jnp
from jax import lax
from jax.experimental import pallas as pl
from jax.experimental.pallas import tpu as pltpu
from jax.sharding import PartitionSpec as P

EPS = 1e-06
MESH = pl.DeviceIdType.MESH
MOST_CHUNKS = 8
AHEAD = 4
HALF = 128


def exchange_kernel(
    n, m, chunks, group_width, scale_rows, scale_blocks, blocks,
    q_in, k_in, v_in, g_in, ex_in, taps_in,
    prod_out, filt_out, peak_out,
    q_ref, k_ref, v_ref, g_ref, ex_ref, taps_ref, sc_ref,
    zs, zf, ws, wr, tt0, tt1, flip_ref, lags, gfs, gfr, peak, pks,
    load_sem, small_sem,
    in_send, in_recv, back_send, back_recv, gf_send, gf_recv, pk_send, pk_recv,
):
    me = lax.axis_index("ctx")
    row_me = lax.axis_index("ch")
    _, own, rows = q_ref.shape
    chunk = own // chunks
    own_groups = own // group_width
    chunk_groups = own_groups // chunks
    filter_len = taps_ref.shape[1]
    lead = filter_len // rows
    cols = filter_len // n
    width = filter_len + HALF
    f32 = jnp.float32
    chips = n // 2

    def flipped(mask):
        out, bit = 0, 1
        while bit < n:
            out = out + lax.rem(lax.div(me, bit) + lax.div(mask, bit), 2) * bit
            bit *= 2
        return out

    core = lax.rem(me, 2)
    peers = []
    for low in range(2):
        for h in range(1, chips):
            swap = (1 if h == 1 else -1 if h == 2 else 0) if chips > 2 else 0
            peers.append(flipped((h + core * swap) * 2 + low))
    peers.append(flipped(jnp.int32(1)))

    loads = tuple(zip((k_in, v_in, q_in, g_in), (k_ref, v_ref, q_ref, g_ref)))

    def load_copy(i, j):
        part = pl.ds(pl.multiple_of(j * chunk, 16), chunk)
        src, dst = loads[i]
        return pltpu.make_async_copy(src.at[:, part, :], dst.at[:, part, :], load_sem.at[i, j])

    ex_copy = pltpu.make_async_copy(ex_in, ex_ref, small_sem.at[0])
    taps_copy = pltpu.make_async_copy(taps_in.at[me], taps_ref, small_sem.at[1])
    ex_copy.start()

    def load_chunk(j, c):
        for i in range(4):
            load_copy(i, j).start()
        return c

    barrier = pltpu.get_barrier_semaphore()

    def greet_ctx(i, c):
        pl.semaphore_signal(
            barrier, inc=1, device_id={"ctx": lax.rem(me + i, n)}, device_id_type=MESH
        )
        return c

    def greet_ch(i, c):
        pl.semaphore_signal(
            barrier, inc=1, device_id={"ch": lax.rem(row_me + i, m)}, device_id_type=MESH
        )
        return c

    lax.fori_loop(1, n, greet_ctx, 0)
    lax.fori_loop(1, m, greet_ch, 0)
    load_chunk(0, 0)
    ex_copy.wait()
    per_scale = rows // blocks
    for a in range(3):
        scale = jnp.exp2(ex_ref[a].astype(f32))
        for i in range(scale_blocks):
            sc_ref[a * scale_blocks + i] = jnp.concatenate(
                [jnp.broadcast_to(scale[b : b + 1, i : i + 1], (1, per_scale)) for b in range(blocks)], axis=1
            )

    def at_rows(owner, j):
        return pl.ds(pl.multiple_of(owner * own + j * chunk, 16), chunk)

    def at_part(j):
        return pl.ds(pl.multiple_of(j * chunk, 16), chunk)

    def scale_of(which, owner, j):
        return sc_ref[which * scale_blocks + (owner * own + j * chunk) // scale_rows]

    def real(ref, which, owner, j):
        return ref[owner, at_part(j), :].astype(f32) * scale_of(which, owner, j)

    def mixed(owner, j):
        z = (real(k_ref, 1, owner, j) * real(v_ref, 2, owner, j)).astype(jnp.bfloat16)
        gw = (real(q_ref, 0, owner, j) * g_ref[owner, at_part(j), :].astype(f32)).astype(jnp.bfloat16)
        return z, gw

    def in_copy(j, dst, src):
        return pltpu.make_async_remote_copy(
            src_ref=zs.at[:, at_rows(dst, j), :],
            dst_ref=zf.at[src, :, pl.ds(pl.multiple_of(j * chunk, 16), chunk), :],
            send_sem=in_send.at[j, dst],
            recv_sem=in_recv.at[j, src],
            device_id={"ctx": dst},
            device_id_type=MESH,
        )

    def back_copy(j, dst, src):
        return pltpu.make_async_remote_copy(
            src_ref=ws.at[dst, :, pl.ds(pl.multiple_of(j * chunk, 16), chunk), :],
            dst_ref=wr.at[:, at_rows(src, j), :],
            send_sem=back_send.at[j, dst],
            recv_sem=back_recv.at[j, src],
            device_id={"ctx": dst},
            device_id_type=MESH,
        )

    def gf_copy(dst, src):
        return pltpu.make_async_remote_copy(
            src_ref=gfs.at[dst],
            dst_ref=gfr.at[src],
            send_sem=gf_send.at[dst],
            recv_sem=gf_recv.at[src],
            device_id={"ctx": dst},
            device_id_type=MESH,
        )

    def pk_copy(dst, src):
        return pltpu.make_async_remote_copy(
            src_ref=pks.at[row_me],
            dst_ref=pks.at[src],
            send_sem=pk_send.at[dst],
            recv_sem=pk_recv.at[src],
            device_id={"ch": dst},
            device_id_type=MESH,
        )

    for i in range(4):
        load_copy(i, 0).wait()
    lax.fori_loop(1, chunks, load_chunk, 0)
    taps_copy.start()
    pl.semaphore_wait(barrier, n - 1 + m - 1)

    def send_chunk(j, c):
        for dst in peers:
            z, gw = mixed(dst, j)
            zs[0, at_rows(dst, j), :] = z
            zs[1, at_rows(dst, j), :] = gw
            in_copy(j, dst, me).start()
        z, gw = mixed(me, j)
        here = pl.ds(pl.multiple_of(j * chunk, 16), chunk)
        zf[me, 0, here, :] = z
        zf[me, 1, here, :] = gw
        return c

    def load_and_send(j, c):
        for i in range(4):
            load_copy(i, j).wait()
        return send_chunk(j, c)

    ahead = min(AHEAD, chunks)
    send_chunk(0, 0)
    lax.fori_loop(1, ahead, load_and_send, 0)

    taps_copy.wait()
    peak[...] = jnp.zeros_like(peak)
    def mirror(size, kind):
        at = lax.broadcasted_iota(jnp.int32, (size, size), 0)
        to = lax.broadcasted_iota(jnp.int32, (size, size), 1)
        return (at + to == size - 1).astype(f32).astype(kind)

    flip_ref[...] = mirror(rows, jnp.bfloat16)
    zero = jnp.zeros((HALF, HALF), jnp.bfloat16)

    def turned(x, by):
        by = (by * group_width) % x.shape[0]
        return x if by == 0 else jnp.concatenate([x[-by:], x[:-by]], axis=0)

    def one_group(gi, tt):
        at = pl.ds(pl.multiple_of(gi * group_width, 16), group_width)
        z = zf[:, 0, at, :].reshape(n * group_width, rows)
        gw = zf[:, 1, at, :].reshape(n * group_width, rows)
        taps = taps_ref[pl.ds(gi, 1), :].astype(jnp.bfloat16).astype(f32)
        line = jnp.concatenate([taps, jnp.zeros((1, HALF), f32)], axis=1)
        band = pltpu.roll(
            jnp.broadcast_to(line, (HALF, width)), 0, 1, stride=1, stride_axis=0
        ).astype(jnp.bfloat16)

        def tile(i):
            if i < 0 or i * HALF >= width:
                return zero
            return band[:, i * HALF : (i + 1) * HALF]

        per = rows // HALF
        for o in range(lead + 1):
            for a in range(per):
                for b in range(per):
                    tt[o * rows + a * HALF : o * rows + (a + 1) * HALF, b * HALF : (b + 1) * HALF] = tile(
                        o * per + b - a
                    )
        gw = jnp.dot(gw, flip_ref[...], preferred_element_type=f32).astype(jnp.bfloat16)
        gparts = [turned(gw, -o) for o in range(lead + 1)]
        both = jnp.concatenate(
            [
                jnp.concatenate([turned(z, o) for o in range(lead + 1)], axis=1),
                jnp.concatenate(gparts, axis=1),
            ],
            axis=0,
        )
        res = jnp.dot(both, tt[...], preferred_element_type=f32).astype(jnp.bfloat16)
        w = res[: n * group_width]
        gz = jnp.dot(res[n * group_width :], flip_ref[...], preferred_element_type=f32)
        ws[:, 0, at, :] = w.reshape(n, group_width, rows)
        ws[:, 1, at, :] = gz.astype(jnp.bfloat16).reshape(n, group_width, rows)

        gwin = jnp.concatenate(gparts[::-1], axis=1)
        zcat = jnp.concatenate([z[:, a * HALF : (a + 1) * HALF] for a in range(per)], axis=0)
        gcat = jnp.concatenate(
            [gwin[:, (per - 1 - a) * HALF : (per - 1 - a) * HALF + width] for a in range(per)], axis=0
        )
        cross = lax.dot_general(zcat, gcat, (((0,), (0,)), ((), ())), preferred_element_type=f32)
        skewed = pltpu.roll(cross, 0, 1, stride=1, stride_axis=0)
        lags[pl.ds(gi, 1), :] = jnp.sum(skewed, axis=0, keepdims=True)[:, HALF:]

    def note_peak(j, owner):
        conv = wr[0, at_rows(owner, j), :].astype(f32)
        gz = wr[1, at_rows(owner, j), :].astype(f32)
        gq = g_ref[owner, at_part(j), :].astype(f32) * conv
        gk = gz * real(v_ref, 2, owner, j)
        gv = gz * real(k_ref, 1, owner, j)
        for i, x in enumerate((gq, gk, gv)):
            prod_out[i, at_rows(owner, j), :] = x
            peak[i] = jnp.maximum(peak[i], jnp.max(jnp.abs(x).reshape(chunk // 8, 8, rows), axis=0))

    def take_back(j):
        for src in peers:
            back_copy(j, me, src).wait_recv()
            note_peak(j, src)
        note_peak(j, me)

    def work_chunk(j, c):
        for src in peers:
            in_copy(j, me, src).wait_recv()
        pl.when(j + ahead < chunks)(lambda: load_and_send(j + ahead, None))
        for u in range(chunk_groups):
            one_group(j * chunk_groups + u, tt1 if u % 2 else tt0)

        for dst in peers:
            back_copy(j, dst, me).start()
        here = pl.ds(pl.multiple_of(j * chunk, 16), chunk)
        for i in range(2):
            wr[i, at_rows(me, j), :] = ws[me, i, here, :]
        return c

    lax.fori_loop(0, chunks, work_chunk, 0)

    back = mirror(HALF, f32)
    straight = jnp.concatenate(
        [
            jnp.dot(
                lags[:, i : i + HALF], back, preferred_element_type=f32, precision=lax.Precision.HIGHEST
            )
            for i in range(filter_len - HALF, -1, -HALF)
        ],
        axis=1,
    )
    for d in range(n):
        gfs[d] = straight[:, d * cols : (d + 1) * cols]

    def send_gf(i, c):
        gf_copy(lax.rem(me + i, n), me).start()
        return c

    lax.fori_loop(1, n, send_gf, 0)

    def take_chunk(j, c):
        take_back(j)
        return c

    lax.fori_loop(0, chunks, take_chunk, 0)

    for i in range(3):
        lanes = jnp.max(peak[i], axis=0, keepdims=True)
        per = rows // blocks
        pks[row_me, i : i + 1, :] = jnp.concatenate(
            [
                jnp.broadcast_to(jnp.max(lanes[:, b * per : (b + 1) * per], axis=1, keepdims=True), (1, per))
                for b in range(blocks)
            ],
            axis=1,
        )
    pks[row_me, 3:8, :] = jnp.zeros((5, rows), f32)

    def send_pk(i, c):
        pk_copy(lax.rem(row_me + i, m), row_me).start()
        return c

    lax.fori_loop(1, m, send_pk, 0)

    gfr[me] = gfs[me]

    def settle_ctx(i, c):
        dst = lax.rem(me + i, n)
        src = lax.rem(me + n - i, n)
        gf_copy(me, src).wait_recv()
        gf_copy(dst, me).wait_send()

        def both(j, c):
            in_copy(j, dst, me).wait_send()
            back_copy(j, dst, me).wait_send()
            return c

        lax.fori_loop(0, chunks, both, 0)
        return c

    lax.fori_loop(1, n, settle_ctx, 0)
    filt_out[...] = gfr[...]

    def settle_ch(i, c):
        pk_copy(row_me, lax.rem(row_me + m - i, m)).wait_recv()
        pk_copy(lax.rem(row_me + i, m), row_me).wait_send()
        return c

    lax.fori_loop(1, m, settle_ch, 0)
    peak_out[...] = jnp.max(pks[...], axis=0)


def scale_kernel(prod, peak, filt, oq, ok, ov, of, op, done, small, sems, small_sems):
    channels, rows = prod.shape[1:]
    blocks = small.shape[0]
    per = rows // blocks
    outs = (oq, ok, ov)
    filt_copy = pltpu.make_async_copy(filt, of, small_sems.at[0])
    filt_copy.start()
    inv = 1.0 / (peak[0:3, :] + EPS)
    step = min(256, channels)

    def out_copy(i, r):
        at = pl.ds(r * step, step)
        return pltpu.make_async_copy(done.at[i, at, :], outs[i].at[at, :], sems.at[i, r])

    for r in range(channels // step):
        for i in range(3):
            at = pl.ds(r * step, step)
            done[i, at, :] = (prod[i, at, :] * inv[i : i + 1]).astype(jnp.bfloat16)
            out_copy(i, r).start()
    at_block = lax.broadcasted_iota(jnp.int32, (blocks, 3), 0)
    at_kind = lax.broadcasted_iota(jnp.int32, (blocks, 3), 1)
    table = jnp.zeros((blocks, 3), jnp.float32)
    for b in range(blocks):
        for i in range(3):
            table = jnp.where(
                (at_block == b) & (at_kind == i), peak[i : i + 1, b * per : b * per + 1], table
            )
    small[...] = table
    peak_copy = pltpu.make_async_copy(small, op, small_sems.at[1])
    peak_copy.start()
    for r in range(channels // step):
        for i in range(3):
            out_copy(i, r).wait()
    filt_copy.wait()
    peak_copy.wait()


def shards(n, m, q_vals, k_vals, v_vals, grad_out, exponents, filter_taps):
    channels, rows = q_vals.shape
    groups, filter_len = filter_taps.shape
    _, scale_blocks, blocks = exponents.shape
    scale_rows = channels // scale_blocks
    group_width = channels // groups
    own = channels // n
    own_groups = groups // n
    chunks = min(MOST_CHUNKS, own_groups)
    cols = filter_len // n
    lead = filter_len // rows
    bf16, f32 = jnp.bfloat16, jnp.float32
    anywhere = pl.BlockSpec(memory_space=pl.ANY)
    vmem = pl.BlockSpec(memory_space=pltpu.VMEM)
    dma = pltpu.SemaphoreType.DMA
    prod, filt, peak = pl.pallas_call(
        functools.partial(exchange_kernel, n, m, chunks, group_width, scale_rows, scale_blocks, blocks),
        out_shape=(
            jax.ShapeDtypeStruct((3, channels, rows), f32),
            jax.ShapeDtypeStruct((n, own_groups, cols), f32),
            jax.ShapeDtypeStruct((8, rows), f32),
        ),
        in_specs=[pl.BlockSpec(memory_space=pltpu.HBM)] * 6,
        out_specs=(vmem, vmem, vmem),
        scratch_shapes=[
            *[pltpu.VMEM((n, own, rows), bf16) for _ in range(4)],
            pltpu.VMEM((3, blocks, scale_blocks), jnp.int32),
            pltpu.VMEM((own_groups, filter_len), f32),
            pltpu.VMEM((3 * scale_blocks, 1, rows), f32),
            pltpu.VMEM((2, channels, rows), bf16),
            pltpu.VMEM((n, 2, own, rows), bf16),
            pltpu.VMEM((n, 2, own, rows), bf16),
            pltpu.VMEM((2, channels, rows), bf16),
            pltpu.VMEM(((lead + 1) * rows, rows), bf16),
            pltpu.VMEM(((lead + 1) * rows, rows), bf16),
            pltpu.VMEM((rows, rows), bf16),
            pltpu.VMEM((own_groups, filter_len), f32),
            pltpu.VMEM((n, own_groups, cols), f32),
            pltpu.VMEM((n, own_groups, cols), f32),
            pltpu.VMEM((3, 8, rows), f32),
            pltpu.VMEM((m, 8, rows), f32),
            dma((4, chunks)),
            dma((2,)),
            dma((chunks, n)),
            dma((chunks, n)),
            dma((chunks, n)),
            dma((chunks, n)),
            dma((n,)),
            dma((n,)),
            dma((m,)),
            dma((m,)),
        ],
        compiler_params=pltpu.CompilerParams(
            collective_id=0, has_side_effects=True, vmem_limit_bytes=32 * 1024 * 1024
        ),
    )(
        *[
            pltpu.with_memory_space_constraint(x, pltpu.HBM)
            for x in (
                *[x.reshape(n, own, rows) for x in (q_vals, k_vals, v_vals, grad_out)],
                exponents.transpose(0, 2, 1),
                filter_taps.reshape(n, own_groups, filter_len),
            )
        ]
    )
    flat = jax.ShapeDtypeStruct((channels, rows), bf16)
    *grads, filt, peak = pl.pallas_call(
        scale_kernel,
        out_shape=(
            flat, flat, flat,
            jax.ShapeDtypeStruct((n, own_groups, cols), f32),
            jax.ShapeDtypeStruct((blocks, 3), f32),
        ),
        in_specs=[vmem] * 3,
        out_specs=[anywhere] * 5,
        scratch_shapes=[
            pltpu.VMEM((3, channels, rows), bf16),
            pltpu.VMEM((blocks, 3), f32),
            dma((3, channels // min(256, channels))),
            dma((2,)),
        ],
        compiler_params=pltpu.CompilerParams(vmem_limit_bytes=16 * 1024 * 1024),
    )(prod, peak, filt)
    return (*grads, filt.reshape(groups, cols), peak.T)


def solution(mesh):
    in_specs = (
        P("ch", "ctx"),
        P("ch", "ctx"),
        P("ch", "ctx"),
        P("ch", "ctx"),
        P(None, "ch", "ctx"),
        P("ch", None),
    )
    out_specs = (P("ch", "ctx"), P("ch", "ctx"), P("ch", "ctx"), P("ch", "ctx"), P(None, "ctx"))
    body = functools.partial(shards, mesh.shape["ctx"], mesh.shape["ch"])
    return jax.shard_map(body, mesh=mesh, in_specs=in_specs, out_specs=out_specs, check_vma=False)
```

```python
import functools

import jax
import jax.numpy as jnp
from jax import lax
from jax.experimental import pallas as pl
from jax.experimental.pallas import tpu as pltpu
from jax.sharding import PartitionSpec as P

EPS = 1e-06
MESH = pl.DeviceIdType.MESH
MOST_CHUNKS = 8
AHEAD = 4
HALF = 128


def exchange_kernel(
    n, m, chunks, group_width, scale_rows, scale_blocks, blocks,
    q_in, k_in, v_in, g_in, ex_in, taps_in,
    prod_out, filt_out, peak_out,
    q_ref, k_ref, v_ref, g_ref, ex_ref, taps_ref, sc_ref,
    zs, zf, ws, wr, tt0, tt1, flip_ref, lags, gfs, gfr, peak, pks,
    rel_in, rel_back, rel_sem, load_sem, small_sem,
    in_send, in_recv, back_send, back_recv, gf_send, gf_recv, pk_send, pk_recv,
):
    me = lax.axis_index("ctx")
    row_me = lax.axis_index("ch")
    _, own, rows = q_ref.shape
    chunk = own // chunks
    own_groups = own // group_width
    chunk_groups = own_groups // chunks
    filter_len = taps_ref.shape[1]
    lead = filter_len // rows
    cols = filter_len // n
    width = filter_len + HALF
    f32 = jnp.float32
    chips = n // 2

    def flipped(mask):
        out, bit = 0, 1
        while bit < n:
            out = out + lax.rem(lax.div(me, bit) + lax.div(mask, bit), 2) * bit
            bit *= 2
        return out

    core = lax.rem(me, 2)
    relayed = chips == 4
    peers = []
    for low in range(2):
        for h in range(1, chips):
            swap = (1 if h == 1 else -1 if h == 2 else 0) if chips > 2 else 0
            if not (relayed and h == 3):
                peers.append(flipped((h + core * swap) * 2 + low))
    peers.append(flipped(jnp.int32(1)))
    direct = list(peers)
    far, onward = [], []
    if relayed:
        via = flipped((1 + core) * 2)
        far = [flipped(jnp.int32(6 + low)) for low in range(2)]
        onward = [flipped((2 - core) * 2 + low) for low in range(2)]
        peers = peers + far

    loads = tuple(zip((k_in, v_in, q_in, g_in), (k_ref, v_ref, q_ref, g_ref)))

    def load_copy(i, j):
        part = pl.ds(pl.multiple_of(j * chunk, 16), chunk)
        src, dst = loads[i]
        return pltpu.make_async_copy(src.at[:, part, :], dst.at[:, part, :], load_sem.at[i, j])

    ex_copy = pltpu.make_async_copy(ex_in, ex_ref, small_sem.at[0])
    taps_copy = pltpu.make_async_copy(taps_in.at[me], taps_ref, small_sem.at[1])
    ex_copy.start()

    def load_chunk(j, c):
        for i in range(4):
            load_copy(i, j).start()
        return c

    barrier = pltpu.get_barrier_semaphore()

    def greet_ctx(i, c):
        pl.semaphore_signal(
            barrier, inc=1, device_id={"ctx": lax.rem(me + i, n)}, device_id_type=MESH
        )
        return c

    def greet_ch(i, c):
        pl.semaphore_signal(
            barrier, inc=1, device_id={"ch": lax.rem(row_me + i, m)}, device_id_type=MESH
        )
        return c

    lax.fori_loop(1, n, greet_ctx, 0)
    lax.fori_loop(1, m, greet_ch, 0)
    load_chunk(0, 0)
    ex_copy.wait()
    per_scale = rows // blocks
    for a in range(3):
        scale = jnp.exp2(ex_ref[a].astype(f32))
        for i in range(scale_blocks):
            sc_ref[a * scale_blocks + i] = jnp.concatenate(
                [jnp.broadcast_to(scale[b : b + 1, i : i + 1], (1, per_scale)) for b in range(blocks)], axis=1
            )

    def at_rows(owner, j):
        return pl.ds(pl.multiple_of(owner * own + j * chunk, 16), chunk)

    def at_part(j):
        return pl.ds(pl.multiple_of(j * chunk, 16), chunk)

    def scale_of(which, owner, j):
        return sc_ref[which * scale_blocks + (owner * own + j * chunk) // scale_rows]

    def real(ref, which, owner, j):
        return ref[owner, at_part(j), :].astype(f32) * scale_of(which, owner, j)

    def mixed(owner, j):
        z = (real(k_ref, 1, owner, j) * real(v_ref, 2, owner, j)).astype(jnp.bfloat16)
        gw = (real(q_ref, 0, owner, j) * g_ref[owner, at_part(j), :].astype(f32)).astype(jnp.bfloat16)
        return z, gw

    def in_copy(j, dst, src):
        return pltpu.make_async_remote_copy(
            src_ref=zs.at[:, at_rows(dst, j), :],
            dst_ref=zf.at[src, :, pl.ds(pl.multiple_of(j * chunk, 16), chunk), :],
            send_sem=in_send.at[j, dst],
            recv_sem=in_recv.at[j, src],
            device_id={"ctx": dst},
            device_id_type=MESH,
        )

    def back_copy(j, dst, src):
        return pltpu.make_async_remote_copy(
            src_ref=ws.at[dst, :, pl.ds(pl.multiple_of(j * chunk, 16), chunk), :],
            dst_ref=wr.at[:, at_rows(src, j), :],
            send_sem=back_send.at[j, dst],
            recv_sem=back_recv.at[j, src],
            device_id={"ctx": dst},
            device_id_type=MESH,
        )

    def in_relay(j, low):
        return pltpu.make_async_remote_copy(
            src_ref=zs.at[:, at_rows(far[low], j), :],
            dst_ref=rel_in.at[j, low],
            send_sem=in_send.at[j, far[low]],
            recv_sem=rel_sem.at[0, j, low],
            device_id={"ctx": via},
            device_id_type=MESH,
        )

    def in_onward(j, low):
        return pltpu.make_async_remote_copy(
            src_ref=rel_in.at[j, low],
            dst_ref=zf.at[via, :, at_part(j), :],
            send_sem=rel_sem.at[1, j, low],
            recv_sem=in_recv.at[j, via],
            device_id={"ctx": onward[low]},
            device_id_type=MESH,
        )

    def back_relay(j, low):
        return pltpu.make_async_remote_copy(
            src_ref=ws.at[far[low], :, at_part(j), :],
            dst_ref=rel_back.at[j, low],
            send_sem=back_send.at[j, far[low]],
            recv_sem=rel_sem.at[2, j, low],
            device_id={"ctx": via},
            device_id_type=MESH,
        )

    def back_onward(j, low):
        return pltpu.make_async_remote_copy(
            src_ref=rel_back.at[j, low],
            dst_ref=wr.at[:, at_rows(via, j), :],
            send_sem=rel_sem.at[3, j, low],
            recv_sem=back_recv.at[j, via],
            device_id={"ctx": onward[low]},
            device_id_type=MESH,
        )

    def pass_in(j):
        for low in range(len(far)):
            in_relay(j, low).wait_recv()
            in_onward(j, low).start()

    def pass_back(j):
        for low in range(len(far)):
            back_relay(j, low).wait_recv()
            back_onward(j, low).start()

    def gf_copy(dst, src):
        return pltpu.make_async_remote_copy(
            src_ref=gfs.at[dst],
            dst_ref=gfr.at[src],
            send_sem=gf_send.at[dst],
            recv_sem=gf_recv.at[src],
            device_id={"ctx": dst},
            device_id_type=MESH,
        )

    def pk_copy(dst, src):
        return pltpu.make_async_remote_copy(
            src_ref=pks.at[row_me],
            dst_ref=pks.at[src],
            send_sem=pk_send.at[dst],
            recv_sem=pk_recv.at[src],
            device_id={"ch": dst},
            device_id_type=MESH,
        )

    for i in range(4):
        load_copy(i, 0).wait()
    lax.fori_loop(1, chunks, load_chunk, 0)
    taps_copy.start()
    pl.semaphore_wait(barrier, n - 1 + m - 1)

    def send_chunk(j, c):
        for low, dst in [*enumerate(far), *((None, d) for d in direct)]:
            z, gw = mixed(dst, j)
            zs[0, at_rows(dst, j), :] = z
            zs[1, at_rows(dst, j), :] = gw
            (in_copy(j, dst, me) if low is None else in_relay(j, low)).start()
        z, gw = mixed(me, j)
        here = pl.ds(pl.multiple_of(j * chunk, 16), chunk)
        zf[me, 0, here, :] = z
        zf[me, 1, here, :] = gw
        return c

    def load_and_send(j, c):
        for i in range(4):
            load_copy(i, j).wait()
        return send_chunk(j, c)

    ahead = min(AHEAD, chunks)
    send_chunk(0, 0)
    lax.fori_loop(1, ahead, load_and_send, 0)

    taps_copy.wait()
    peak[...] = jnp.zeros_like(peak)
    def mirror(size, kind):
        at = lax.broadcasted_iota(jnp.int32, (size, size), 0)
        to = lax.broadcasted_iota(jnp.int32, (size, size), 1)
        return (at + to == size - 1).astype(f32).astype(kind)

    flip_ref[...] = mirror(rows, jnp.bfloat16)
    zero = jnp.zeros((HALF, HALF), jnp.bfloat16)

    def turned(x, by):
        by = (by * group_width) % x.shape[0]
        return x if by == 0 else jnp.concatenate([x[-by:], x[:-by]], axis=0)

    def one_group(gi, tt):
        at = pl.ds(pl.multiple_of(gi * group_width, 16), group_width)
        z = zf[:, 0, at, :].reshape(n * group_width, rows)
        gw = zf[:, 1, at, :].reshape(n * group_width, rows)
        taps = taps_ref[pl.ds(gi, 1), :].astype(jnp.bfloat16).astype(f32)
        line = jnp.concatenate([taps, jnp.zeros((1, HALF), f32)], axis=1)
        band = pltpu.roll(
            jnp.broadcast_to(line, (HALF, width)), 0, 1, stride=1, stride_axis=0
        ).astype(jnp.bfloat16)

        def tile(i):
            if i < 0 or i * HALF >= width:
                return zero
            return band[:, i * HALF : (i + 1) * HALF]

        per = rows // HALF
        for o in range(lead + 1):
            for a in range(per):
                for b in range(per):
                    tt[o * rows + a * HALF : o * rows + (a + 1) * HALF, b * HALF : (b + 1) * HALF] = tile(
                        o * per + b - a
                    )
        gw = jnp.dot(gw, flip_ref[...], preferred_element_type=f32).astype(jnp.bfloat16)
        gparts = [turned(gw, -o) for o in range(lead + 1)]
        both = jnp.concatenate(
            [
                jnp.concatenate([turned(z, o) for o in range(lead + 1)], axis=1),
                jnp.concatenate(gparts, axis=1),
            ],
            axis=0,
        )
        res = jnp.dot(both, tt[...], preferred_element_type=f32).astype(jnp.bfloat16)
        w = res[: n * group_width]
        gz = jnp.dot(res[n * group_width :], flip_ref[...], preferred_element_type=f32)
        ws[:, 0, at, :] = w.reshape(n, group_width, rows)
        ws[:, 1, at, :] = gz.astype(jnp.bfloat16).reshape(n, group_width, rows)

        gwin = jnp.concatenate(gparts[::-1], axis=1)
        zcat = jnp.concatenate([z[:, a * HALF : (a + 1) * HALF] for a in range(per)], axis=0)
        gcat = jnp.concatenate(
            [gwin[:, (per - 1 - a) * HALF : (per - 1 - a) * HALF + width] for a in range(per)], axis=0
        )
        cross = lax.dot_general(zcat, gcat, (((0,), (0,)), ((), ())), preferred_element_type=f32)
        skewed = pltpu.roll(cross, 0, 1, stride=1, stride_axis=0)
        lags[pl.ds(gi, 1), :] = jnp.sum(skewed, axis=0, keepdims=True)[:, HALF:]

    def note_peak(j, owner):
        conv = wr[0, at_rows(owner, j), :].astype(f32)
        gz = wr[1, at_rows(owner, j), :].astype(f32)
        gq = g_ref[owner, at_part(j), :].astype(f32) * conv
        gk = gz * real(v_ref, 2, owner, j)
        gv = gz * real(k_ref, 1, owner, j)
        for i, x in enumerate((gq, gk, gv)):
            prod_out[i, at_rows(owner, j), :] = x
            peak[i] = jnp.maximum(peak[i], jnp.max(jnp.abs(x).reshape(chunk // 8, 8, rows), axis=0))

    def take_back(j):
        for src in peers:
            back_copy(j, me, src).wait_recv()
            note_peak(j, src)
        note_peak(j, me)

    def work_chunk(j, c):
        for src in peers:
            in_copy(j, me, src).wait_recv()
        pl.when(j + ahead < chunks)(lambda: load_and_send(j + ahead, None))
        for u in range(chunk_groups):
            one_group(j * chunk_groups + u, tt1 if u % 2 else tt0)
            if u == 0:
                pl.when(j + 1 < chunks)(lambda: pass_in(j + 1))
                pl.when(j > 0)(lambda: pass_back(j - 1))

        for low in range(len(far)):
            back_relay(j, low).start()
        for dst in direct:
            back_copy(j, dst, me).start()
        here = pl.ds(pl.multiple_of(j * chunk, 16), chunk)
        for i in range(2):
            wr[i, at_rows(me, j), :] = ws[me, i, here, :]
        return c

    pass_in(0)
    lax.fori_loop(0, chunks, work_chunk, 0)
    pass_back(chunks - 1)

    back = mirror(HALF, f32)
    straight = jnp.concatenate(
        [
            jnp.dot(
                lags[:, i : i + HALF], back, preferred_element_type=f32, precision=lax.Precision.HIGHEST
            )
            for i in range(filter_len - HALF, -1, -HALF)
        ],
        axis=1,
    )
    for d in range(n):
        gfs[d] = straight[:, d * cols : (d + 1) * cols]

    def send_gf(i, c):
        gf_copy(lax.rem(me + i, n), me).start()
        return c

    lax.fori_loop(1, n, send_gf, 0)

    def take_chunk(j, c):
        take_back(j)
        return c

    lax.fori_loop(0, chunks, take_chunk, 0)

    for i in range(3):
        lanes = jnp.max(peak[i], axis=0, keepdims=True)
        per = rows // blocks
        pks[row_me, i : i + 1, :] = jnp.concatenate(
            [
                jnp.broadcast_to(jnp.max(lanes[:, b * per : (b + 1) * per], axis=1, keepdims=True), (1, per))
                for b in range(blocks)
            ],
            axis=1,
        )
    pks[row_me, 3:8, :] = jnp.zeros((5, rows), f32)

    def send_pk(i, c):
        pk_copy(lax.rem(row_me + i, m), row_me).start()
        return c

    lax.fori_loop(1, m, send_pk, 0)

    gfr[me] = gfs[me]

    def settle_relay(j, c):
        for low in range(len(far)):
            in_onward(j, low).wait_send()
            back_onward(j, low).wait_send()
        return c

    lax.fori_loop(0, chunks, settle_relay, 0)

    def settle_ctx(i, c):
        dst = lax.rem(me + i, n)
        src = lax.rem(me + n - i, n)
        gf_copy(me, src).wait_recv()
        gf_copy(dst, me).wait_send()

        def both(j, c):
            in_copy(j, dst, me).wait_send()
            back_copy(j, dst, me).wait_send()
            return c

        lax.fori_loop(0, chunks, both, 0)
        return c

    lax.fori_loop(1, n, settle_ctx, 0)
    filt_out[...] = gfr[...]

    def settle_ch(i, c):
        pk_copy(row_me, lax.rem(row_me + m - i, m)).wait_recv()
        pk_copy(lax.rem(row_me + i, m), row_me).wait_send()
        return c

    lax.fori_loop(1, m, settle_ch, 0)
    peak_out[...] = jnp.max(pks[...], axis=0)


def scale_kernel(prod, peak, filt, oq, ok, ov, of, op, done, small, sems, small_sems):
    channels, rows = prod.shape[1:]
    blocks = small.shape[0]
    per = rows // blocks
    outs = (oq, ok, ov)
    filt_copy = pltpu.make_async_copy(filt, of, small_sems.at[0])
    filt_copy.start()
    inv = 1.0 / (peak[0:3, :] + EPS)
    step = min(256, channels)

    def out_copy(i, r):
        at = pl.ds(r * step, step)
        return pltpu.make_async_copy(done.at[i, at, :], outs[i].at[at, :], sems.at[i, r])

    for r in range(channels // step):
        for i in range(3):
            at = pl.ds(r * step, step)
            done[i, at, :] = (prod[i, at, :] * inv[i : i + 1]).astype(jnp.bfloat16)
            out_copy(i, r).start()
    at_block = lax.broadcasted_iota(jnp.int32, (blocks, 3), 0)
    at_kind = lax.broadcasted_iota(jnp.int32, (blocks, 3), 1)
    table = jnp.zeros((blocks, 3), jnp.float32)
    for b in range(blocks):
        for i in range(3):
            table = jnp.where(
                (at_block == b) & (at_kind == i), peak[i : i + 1, b * per : b * per + 1], table
            )
    small[...] = table
    peak_copy = pltpu.make_async_copy(small, op, small_sems.at[1])
    peak_copy.start()
    for r in range(channels // step):
        for i in range(3):
            out_copy(i, r).wait()
    filt_copy.wait()
    peak_copy.wait()


def shards(n, m, q_vals, k_vals, v_vals, grad_out, exponents, filter_taps):
    channels, rows = q_vals.shape
    groups, filter_len = filter_taps.shape
    _, scale_blocks, blocks = exponents.shape
    scale_rows = channels // scale_blocks
    group_width = channels // groups
    own = channels // n
    own_groups = groups // n
    chunks = min(MOST_CHUNKS, own_groups)
    cols = filter_len // n
    lead = filter_len // rows
    bf16, f32 = jnp.bfloat16, jnp.float32
    anywhere = pl.BlockSpec(memory_space=pl.ANY)
    vmem = pl.BlockSpec(memory_space=pltpu.VMEM)
    dma = pltpu.SemaphoreType.DMA
    prod, filt, peak = pl.pallas_call(
        functools.partial(exchange_kernel, n, m, chunks, group_width, scale_rows, scale_blocks, blocks),
        out_shape=(
            jax.ShapeDtypeStruct((3, channels, rows), f32),
            jax.ShapeDtypeStruct((n, own_groups, cols), f32),
            jax.ShapeDtypeStruct((8, rows), f32),
        ),
        in_specs=[pl.BlockSpec(memory_space=pltpu.HBM)] * 6,
        out_specs=(vmem, vmem, vmem),
        scratch_shapes=[
            *[pltpu.VMEM((n, own, rows), bf16) for _ in range(4)],
            pltpu.VMEM((3, blocks, scale_blocks), jnp.int32),
            pltpu.VMEM((own_groups, filter_len), f32),
            pltpu.VMEM((3 * scale_blocks, 1, rows), f32),
            pltpu.VMEM((2, channels, rows), bf16),
            pltpu.VMEM((n, 2, own, rows), bf16),
            pltpu.VMEM((n, 2, own, rows), bf16),
            pltpu.VMEM((2, channels, rows), bf16),
            pltpu.VMEM(((lead + 1) * rows, rows), bf16),
            pltpu.VMEM(((lead + 1) * rows, rows), bf16),
            pltpu.VMEM((rows, rows), bf16),
            pltpu.VMEM((own_groups, filter_len), f32),
            pltpu.VMEM((n, own_groups, cols), f32),
            pltpu.VMEM((n, own_groups, cols), f32),
            pltpu.VMEM((3, 8, rows), f32),
            pltpu.VMEM((m, 8, rows), f32),
            pltpu.VMEM((chunks, 2, 2, own // chunks, rows), bf16),
            pltpu.VMEM((chunks, 2, 2, own // chunks, rows), bf16),
            dma((4, chunks, 2)),
            dma((4, chunks)),
            dma((2,)),
            dma((chunks, n)),
            dma((chunks, n)),
            dma((chunks, n)),
            dma((chunks, n)),
            dma((n,)),
            dma((n,)),
            dma((m,)),
            dma((m,)),
        ],
        compiler_params=pltpu.CompilerParams(
            collective_id=0, has_side_effects=True, vmem_limit_bytes=32 * 1024 * 1024
        ),
    )(
        *[
            pltpu.with_memory_space_constraint(x, pltpu.HBM)
            for x in (
                *[x.reshape(n, own, rows) for x in (q_vals, k_vals, v_vals, grad_out)],
                exponents.transpose(0, 2, 1),
                filter_taps.reshape(n, own_groups, filter_len),
            )
        ]
    )
    flat = jax.ShapeDtypeStruct((channels, rows), bf16)
    *grads, filt, peak = pl.pallas_call(
        scale_kernel,
        out_shape=(
            flat, flat, flat,
            jax.ShapeDtypeStruct((n, own_groups, cols), f32),
            jax.ShapeDtypeStruct((blocks, 3), f32),
        ),
        in_specs=[vmem] * 3,
        out_specs=[anywhere] * 5,
        scratch_shapes=[
            pltpu.VMEM((3, channels, rows), bf16),
            pltpu.VMEM((blocks, 3), f32),
            dma((3, channels // min(256, channels))),
            dma((2,)),
        ],
        compiler_params=pltpu.CompilerParams(vmem_limit_bytes=16 * 1024 * 1024),
    )(prod, peak, filt)
    return (*grads, filt.reshape(groups, cols), peak.T)


def solution(mesh):
    in_specs = (
        P("ch", "ctx"),
        P("ch", "ctx"),
        P("ch", "ctx"),
        P("ch", "ctx"),
        P(None, "ch", "ctx"),
        P("ch", None),
    )
    out_specs = (P("ch", "ctx"), P("ch", "ctx"), P("ch", "ctx"), P("ch", "ctx"), P(None, "ctx"))
    body = functools.partial(shards, mesh.shape["ctx"], mesh.shape["ch"])
    return jax.shard_map(body, mesh=mesh, in_specs=in_specs, out_specs=out_specs, check_vma=False)
```

```python
import functools

import jax
import jax.numpy as jnp
from jax import lax
from jax.experimental import pallas as pl
from jax.experimental.pallas import tpu as pltpu
from jax.sharding import PartitionSpec as P

EPS = 1e-06
MESH = pl.DeviceIdType.MESH
MOST_CHUNKS = 8
HALF = 128


def exchange_kernel(
    n, m, chunks, group_width, scale_rows, scale_blocks, blocks,
    q_in, k_in, v_in, g_in, ex_in, taps_in,
    prod_out, filt_out, peak_out,
    q_ref, k_ref, v_ref, g_ref, ex_ref, taps_ref, sc_ref,
    zs, zf, ws, wr, tt0, tt1, flip_ref, lags, gfs, gfr, peak, pks,
    load_sem, small_sem,
    in_send, in_recv, back_send, back_recv, gf_send, gf_recv, pk_send, pk_recv,
):
    me = lax.axis_index("ctx")
    row_me = lax.axis_index("ch")
    _, own, rows = q_ref.shape
    chunk = own // chunks
    own_groups = own // group_width
    chunk_groups = own_groups // chunks
    filter_len = taps_ref.shape[1]
    lead = filter_len // rows
    cols = filter_len // n
    width = filter_len + HALF
    f32 = jnp.float32
    chips = n // 2

    def flipped(mask):
        out, bit = 0, 1
        while bit < n:
            out = out + lax.rem(lax.div(me, bit) + lax.div(mask, bit), 2) * bit
            bit *= 2
        return out

    core = lax.rem(me, 2)
    one_hop = [flipped(jnp.int32(x)) for x in ((4, 5) if chips == 4 else ())]
    others = [flipped(jnp.int32(x)) for x in ((2, 6, 3, 7) if chips == 4 else range(2, n))]
    mate = flipped(jnp.int32(1))
    peers = one_hop + others + [mate]

    def by_core(even, odd, act):
        for parity, dsts in ((0, even), (1, odd)):

            @pl.when(core == parity)
            def _(dsts=dsts):
                for dst in dsts:
                    act(dst)

    def over_chunks(act):
        def one(j, c):
            act(j)
            return c

        lax.fori_loop(0, chunks, one, 0)

    loads = tuple(zip((k_in, v_in, q_in, g_in), (k_ref, v_ref, q_ref, g_ref)))

    def load_copy(i, j):
        part = pl.ds(pl.multiple_of(j * chunk, 16), chunk)
        src, dst = loads[i]
        return pltpu.make_async_copy(src.at[:, part, :], dst.at[:, part, :], load_sem.at[i, j])

    ex_copy = pltpu.make_async_copy(ex_in, ex_ref, small_sem.at[0])
    taps_copy = pltpu.make_async_copy(taps_in.at[me], taps_ref, small_sem.at[1])
    ex_copy.start()

    def load_chunk(j, c):
        for i in range(4):
            load_copy(i, j).start()
        return c

    barrier = pltpu.get_barrier_semaphore()

    def greet_ctx(i, c):
        pl.semaphore_signal(
            barrier, inc=1, device_id={"ctx": lax.rem(me + i, n)}, device_id_type=MESH
        )
        return c

    def greet_ch(i, c):
        pl.semaphore_signal(
            barrier, inc=1, device_id={"ch": lax.rem(row_me + i, m)}, device_id_type=MESH
        )
        return c

    lax.fori_loop(1, n, greet_ctx, 0)
    lax.fori_loop(1, m, greet_ch, 0)
    lax.fori_loop(0, chunks, load_chunk, 0)
    taps_copy.start()
    ex_copy.wait()
    per_scale = rows // blocks
    for a in range(3):
        scale = jnp.exp2(ex_ref[a].astype(f32))
        for i in range(scale_blocks):
            sc_ref[a * scale_blocks + i] = jnp.concatenate(
                [jnp.broadcast_to(scale[b : b + 1, i : i + 1], (1, per_scale)) for b in range(blocks)], axis=1
            )

    def at_rows(owner, j):
        return pl.ds(pl.multiple_of(owner * own + j * chunk, 16), chunk)

    def at_part(j):
        return pl.ds(pl.multiple_of(j * chunk, 16), chunk)

    def scale_of(which, owner, j):
        return sc_ref[which * scale_blocks + (owner * own + j * chunk) // scale_rows]

    def real(ref, which, owner, j):
        return ref[owner, at_part(j), :].astype(f32) * scale_of(which, owner, j)

    def mixed(owner, j):
        z = (real(k_ref, 1, owner, j) * real(v_ref, 2, owner, j)).astype(jnp.bfloat16)
        gw = (real(q_ref, 0, owner, j) * g_ref[owner, at_part(j), :].astype(f32)).astype(jnp.bfloat16)
        return z, gw

    def in_copy(j, dst, src):
        return pltpu.make_async_remote_copy(
            src_ref=zs.at[:, at_rows(dst, j), :],
            dst_ref=zf.at[src, :, pl.ds(pl.multiple_of(j * chunk, 16), chunk), :],
            send_sem=in_send.at[j, dst],
            recv_sem=in_recv.at[j, src],
            device_id={"ctx": dst},
            device_id_type=MESH,
        )

    def back_copy(j, dst, src):
        return pltpu.make_async_remote_copy(
            src_ref=ws.at[dst, :, pl.ds(pl.multiple_of(j * chunk, 16), chunk), :],
            dst_ref=wr.at[:, at_rows(src, j), :],
            send_sem=back_send.at[j, dst],
            recv_sem=back_recv.at[j, src],
            device_id={"ctx": dst},
            device_id_type=MESH,
        )

    def gf_copy(dst, src):
        return pltpu.make_async_remote_copy(
            src_ref=gfs.at[dst],
            dst_ref=gfr.at[src],
            send_sem=gf_send.at[dst],
            recv_sem=gf_recv.at[src],
            device_id={"ctx": dst},
            device_id_type=MESH,
        )

    def pk_copy(dst, src):
        return pltpu.make_async_remote_copy(
            src_ref=pks.at[row_me],
            dst_ref=pks.at[src],
            send_sem=pk_send.at[dst],
            recv_sem=pk_recv.at[src],
            device_id={"ch": dst},
            device_id_type=MESH,
        )

    pl.semaphore_wait(barrier, n - 1 + m - 1)

    def send_chunk(j, c):
        for i in range(4):
            load_copy(i, j).wait()

        for dst in peers:
            z, gw = mixed(dst, j)
            zs[0, at_rows(dst, j), :] = z
            zs[1, at_rows(dst, j), :] = gw
        by_core(one_hop, others, lambda dst: in_copy(j, dst, me).start())
        in_copy(j, mate, me).start()
        z, gw = mixed(me, j)
        here = pl.ds(pl.multiple_of(j * chunk, 16), chunk)
        zf[me, 0, here, :] = z
        zf[me, 1, here, :] = gw
        return c

    lax.fori_loop(0, chunks, send_chunk, 0)
    over_chunks(lambda j: by_core(one_hop, others, lambda dst: in_copy(j, dst, me).wait_send()))
    over_chunks(lambda j: by_core(others, one_hop, lambda dst: in_copy(j, dst, me).start()))

    taps_copy.wait()
    peak[...] = jnp.zeros_like(peak)
    def mirror(size, kind):
        at = lax.broadcasted_iota(jnp.int32, (size, size), 0)
        to = lax.broadcasted_iota(jnp.int32, (size, size), 1)
        return (at + to == size - 1).astype(f32).astype(kind)

    flip_ref[...] = mirror(rows, jnp.bfloat16)
    zero = jnp.zeros((HALF, HALF), jnp.bfloat16)

    def turned(x, by):
        by = (by * group_width) % x.shape[0]
        return x if by == 0 else jnp.concatenate([x[-by:], x[:-by]], axis=0)

    def one_group(gi, tt):
        at = pl.ds(pl.multiple_of(gi * group_width, 16), group_width)
        z = zf[:, 0, at, :].reshape(n * group_width, rows)
        gw = zf[:, 1, at, :].reshape(n * group_width, rows)
        taps = taps_ref[pl.ds(gi, 1), :].astype(jnp.bfloat16).astype(f32)
        line = jnp.concatenate([taps, jnp.zeros((1, HALF), f32)], axis=1)
        band = pltpu.roll(
            jnp.broadcast_to(line, (HALF, width)), 0, 1, stride=1, stride_axis=0
        ).astype(jnp.bfloat16)

        def tile(i):
            if i < 0 or i * HALF >= width:
                return zero
            return band[:, i * HALF : (i + 1) * HALF]

        per = rows // HALF
        for o in range(lead + 1):
            for a in range(per):
                for b in range(per):
                    tt[o * rows + a * HALF : o * rows + (a + 1) * HALF, b * HALF : (b + 1) * HALF] = tile(
                        o * per + b - a
                    )
        gw = jnp.dot(gw, flip_ref[...], preferred_element_type=f32).astype(jnp.bfloat16)
        gparts = [turned(gw, -o) for o in range(lead + 1)]
        both = jnp.concatenate(
            [
                jnp.concatenate([turned(z, o) for o in range(lead + 1)], axis=1),
                jnp.concatenate(gparts, axis=1),
            ],
            axis=0,
        )
        res = jnp.dot(both, tt[...], preferred_element_type=f32).astype(jnp.bfloat16)
        w = res[: n * group_width]
        gz = jnp.dot(res[n * group_width :], flip_ref[...], preferred_element_type=f32)
        ws[:, 0, at, :] = w.reshape(n, group_width, rows)
        ws[:, 1, at, :] = gz.astype(jnp.bfloat16).reshape(n, group_width, rows)

        gwin = jnp.concatenate(gparts[::-1], axis=1)
        zcat = jnp.concatenate([z[:, a * HALF : (a + 1) * HALF] for a in range(per)], axis=0)
        gcat = jnp.concatenate(
            [gwin[:, (per - 1 - a) * HALF : (per - 1 - a) * HALF + width] for a in range(per)], axis=0
        )
        cross = lax.dot_general(zcat, gcat, (((0,), (0,)), ((), ())), preferred_element_type=f32)
        skewed = pltpu.roll(cross, 0, 1, stride=1, stride_axis=0)
        lags[pl.ds(gi, 1), :] = jnp.sum(skewed, axis=0, keepdims=True)[:, HALF:]

    def note_peak(j, owner):
        conv = wr[0, at_rows(owner, j), :].astype(f32)
        gz = wr[1, at_rows(owner, j), :].astype(f32)
        gq = g_ref[owner, at_part(j), :].astype(f32) * conv
        gk = gz * real(v_ref, 2, owner, j)
        gv = gz * real(k_ref, 1, owner, j)
        for i, x in enumerate((gq, gk, gv)):
            prod_out[i, at_rows(owner, j), :] = x
            peak[i] = jnp.maximum(peak[i], jnp.max(jnp.abs(x).reshape(chunk // 8, 8, rows), axis=0))

    def take_back(j):
        for src in peers:
            back_copy(j, me, src).wait_recv()
            note_peak(j, src)
        note_peak(j, me)

    def work_chunk(j, c):
        for src in peers:
            in_copy(j, me, src).wait_recv()
        for u in range(chunk_groups):
            one_group(j * chunk_groups + u, tt1 if u % 2 else tt0)

        by_core(others, one_hop, lambda dst: back_copy(j, dst, me).start())
        back_copy(j, mate, me).start()
        here = pl.ds(pl.multiple_of(j * chunk, 16), chunk)
        for i in range(2):
            wr[i, at_rows(me, j), :] = ws[me, i, here, :]
        return c

    lax.fori_loop(0, chunks, work_chunk, 0)
    over_chunks(lambda j: by_core(others, one_hop, lambda dst: back_copy(j, dst, me).wait_send()))
    over_chunks(lambda j: by_core(one_hop, others, lambda dst: back_copy(j, dst, me).start()))

    back = mirror(HALF, f32)
    straight = jnp.concatenate(
        [
            jnp.dot(
                lags[:, i : i + HALF], back, preferred_element_type=f32, precision=lax.Precision.HIGHEST
            )
            for i in range(filter_len - HALF, -1, -HALF)
        ],
        axis=1,
    )
    for d in range(n):
        gfs[d] = straight[:, d * cols : (d + 1) * cols]

    def send_gf(i, c):
        gf_copy(lax.rem(me + i, n), me).start()
        return c

    lax.fori_loop(1, n, send_gf, 0)

    def take_chunk(j, c):
        take_back(j)
        return c

    lax.fori_loop(0, chunks, take_chunk, 0)

    for i in range(3):
        lanes = jnp.max(peak[i], axis=0, keepdims=True)
        per = rows // blocks
        pks[row_me, i : i + 1, :] = jnp.concatenate(
            [
                jnp.broadcast_to(jnp.max(lanes[:, b * per : (b + 1) * per], axis=1, keepdims=True), (1, per))
                for b in range(blocks)
            ],
            axis=1,
        )
    pks[row_me, 3:8, :] = jnp.zeros((5, rows), f32)

    def send_pk(i, c):
        pk_copy(lax.rem(row_me + i, m), row_me).start()
        return c

    lax.fori_loop(1, m, send_pk, 0)

    gfr[me] = gfs[me]

    def settle_ctx(i, c):
        dst = lax.rem(me + i, n)
        src = lax.rem(me + n - i, n)
        gf_copy(me, src).wait_recv()
        gf_copy(dst, me).wait_send()

        return c

    lax.fori_loop(1, n, settle_ctx, 0)
    over_chunks(lambda j: by_core(others, one_hop, lambda dst: in_copy(j, dst, me).wait_send()))
    over_chunks(lambda j: by_core(one_hop, others, lambda dst: back_copy(j, dst, me).wait_send()))

    def settle_mate(j):
        in_copy(j, mate, me).wait_send()
        back_copy(j, mate, me).wait_send()

    over_chunks(settle_mate)
    filt_out[...] = gfr[...]

    def settle_ch(i, c):
        pk_copy(row_me, lax.rem(row_me + m - i, m)).wait_recv()
        pk_copy(lax.rem(row_me + i, m), row_me).wait_send()
        return c

    lax.fori_loop(1, m, settle_ch, 0)
    peak_out[...] = jnp.max(pks[...], axis=0)


def scale_kernel(prod, peak, filt, oq, ok, ov, of, op, done, small, sems, small_sems):
    channels, rows = prod.shape[1:]
    blocks = small.shape[0]
    per = rows // blocks
    outs = (oq, ok, ov)
    filt_copy = pltpu.make_async_copy(filt, of, small_sems.at[0])
    filt_copy.start()
    inv = 1.0 / (peak[0:3, :] + EPS)
    step = min(256, channels)

    def out_copy(i, r):
        at = pl.ds(r * step, step)
        return pltpu.make_async_copy(done.at[i, at, :], outs[i].at[at, :], sems.at[i, r])

    for r in range(channels // step):
        for i in range(3):
            at = pl.ds(r * step, step)
            done[i, at, :] = (prod[i, at, :] * inv[i : i + 1]).astype(jnp.bfloat16)
            out_copy(i, r).start()
    at_block = lax.broadcasted_iota(jnp.int32, (blocks, 3), 0)
    at_kind = lax.broadcasted_iota(jnp.int32, (blocks, 3), 1)
    table = jnp.zeros((blocks, 3), jnp.float32)
    for b in range(blocks):
        for i in range(3):
            table = jnp.where(
                (at_block == b) & (at_kind == i), peak[i : i + 1, b * per : b * per + 1], table
            )
    small[...] = table
    peak_copy = pltpu.make_async_copy(small, op, small_sems.at[1])
    peak_copy.start()
    for r in range(channels // step):
        for i in range(3):
            out_copy(i, r).wait()
    filt_copy.wait()
    peak_copy.wait()


def shards(n, m, q_vals, k_vals, v_vals, grad_out, exponents, filter_taps):
    channels, rows = q_vals.shape
    groups, filter_len = filter_taps.shape
    _, scale_blocks, blocks = exponents.shape
    scale_rows = channels // scale_blocks
    group_width = channels // groups
    own = channels // n
    own_groups = groups // n
    chunks = min(MOST_CHUNKS, own_groups)
    cols = filter_len // n
    lead = filter_len // rows
    bf16, f32 = jnp.bfloat16, jnp.float32
    anywhere = pl.BlockSpec(memory_space=pl.ANY)
    vmem = pl.BlockSpec(memory_space=pltpu.VMEM)
    dma = pltpu.SemaphoreType.DMA
    prod, filt, peak = pl.pallas_call(
        functools.partial(exchange_kernel, n, m, chunks, group_width, scale_rows, scale_blocks, blocks),
        out_shape=(
            jax.ShapeDtypeStruct((3, channels, rows), f32),
            jax.ShapeDtypeStruct((n, own_groups, cols), f32),
            jax.ShapeDtypeStruct((8, rows), f32),
        ),
        in_specs=[pl.BlockSpec(memory_space=pltpu.HBM)] * 6,
        out_specs=(vmem, vmem, vmem),
        scratch_shapes=[
            *[pltpu.VMEM((n, own, rows), bf16) for _ in range(4)],
            pltpu.VMEM((3, blocks, scale_blocks), jnp.int32),
            pltpu.VMEM((own_groups, filter_len), f32),
            pltpu.VMEM((3 * scale_blocks, 1, rows), f32),
            pltpu.VMEM((2, channels, rows), bf16),
            pltpu.VMEM((n, 2, own, rows), bf16),
            pltpu.VMEM((n, 2, own, rows), bf16),
            pltpu.VMEM((2, channels, rows), bf16),
            pltpu.VMEM(((lead + 1) * rows, rows), bf16),
            pltpu.VMEM(((lead + 1) * rows, rows), bf16),
            pltpu.VMEM((rows, rows), bf16),
            pltpu.VMEM((own_groups, filter_len), f32),
            pltpu.VMEM((n, own_groups, cols), f32),
            pltpu.VMEM((n, own_groups, cols), f32),
            pltpu.VMEM((3, 8, rows), f32),
            pltpu.VMEM((m, 8, rows), f32),
            dma((4, chunks)),
            dma((2,)),
            dma((chunks, n)),
            dma((chunks, n)),
            dma((chunks, n)),
            dma((chunks, n)),
            dma((n,)),
            dma((n,)),
            dma((m,)),
            dma((m,)),
        ],
        compiler_params=pltpu.CompilerParams(
            collective_id=0, has_side_effects=True, vmem_limit_bytes=32 * 1024 * 1024
        ),
    )(
        *[
            pltpu.with_memory_space_constraint(x, pltpu.HBM)
            for x in (
                *[x.reshape(n, own, rows) for x in (q_vals, k_vals, v_vals, grad_out)],
                exponents.transpose(0, 2, 1),
                filter_taps.reshape(n, own_groups, filter_len),
            )
        ]
    )
    flat = jax.ShapeDtypeStruct((channels, rows), bf16)
    *grads, filt, peak = pl.pallas_call(
        scale_kernel,
        out_shape=(
            flat, flat, flat,
            jax.ShapeDtypeStruct((n, own_groups, cols), f32),
            jax.ShapeDtypeStruct((blocks, 3), f32),
        ),
        in_specs=[vmem] * 3,
        out_specs=[anywhere] * 5,
        scratch_shapes=[
            pltpu.VMEM((3, channels, rows), bf16),
            pltpu.VMEM((blocks, 3), f32),
            dma((3, channels // min(256, channels))),
            dma((2,)),
        ],
        compiler_params=pltpu.CompilerParams(vmem_limit_bytes=16 * 1024 * 1024),
    )(prod, peak, filt)
    return (*grads, filt.reshape(groups, cols), peak.T)


def solution(mesh):
    in_specs = (
        P("ch", "ctx"),
        P("ch", "ctx"),
        P("ch", "ctx"),
        P("ch", "ctx"),
        P(None, "ch", "ctx"),
        P("ch", None),
    )
    out_specs = (P("ch", "ctx"), P("ch", "ctx"), P("ch", "ctx"), P("ch", "ctx"), P(None, "ctx"))
    body = functools.partial(shards, mesh.shape["ctx"], mesh.shape["ch"])
    return jax.shard_map(body, mesh=mesh, in_specs=in_specs, out_specs=out_specs, check_vma=False)
```
